1024 devices in a mesh: batch: 32 (over z, x_hi), mp: 32 (over y, x_lo, core).
Axes of the slice: x: 4 (x_hi: 2, x_lo: 2; x = x_hi * 2 + x_lo), y: 8, z: 16, core: 2. Of those that a mesh axis runs over, the one named last changes fastest.
Arguments:
- images: bfloat16 [1152, 262144], P('mp', 'batch'), may hold values from -0.25 to 0.25
- texts: bfloat16 [262144, 1152], P(('batch', 'mp')), may hold values from -0.25 to 0.25
- positive: int32 [262144], P(('batch', 'mp')), may hold values from 0 to 1023
- log_scale: float32 [1], replicated, may hold values from 2 to 2.6
- bias: float32 [1], replicated, may hold values from -3 to -1
Outputs:
- loss_rows: float32 [262144], P(('batch', 'mp'))
- image_grad: bfloat16 [1152, 262144], P('mp', 'batch')
- text_grad: float32 [262144, 1152], P(('batch', 'mp'))
The draws below stay inside these ranges and needn't reach their ends.
All inputs are finite; a program needn't handle non-finite values.
Results may differ from the reference program's by a relative error of at most 0.011.
Values may be sent and summed in bfloat16 or wider, within the bound.
No kernel may reach another device: no remote copies, remote signals or barrier semaphores. Data moves between devices by JAX's collectives and lax.ppermute only.
A program may use at most 32 MiB of HBM per device.

```python
import jax
import jax.numpy as jnp
from jax import lax

D = 1152
ROWS = 256
STEPS = 4
IMAGES = 262144
TEXTS = 262144
N_BATCH = 32
N_MP = 32


def set_ends(result, own_key, smallest, largest):
    shape = result.shape
    place = [jax.random.randint(jax.random.fold_in(own_key, axis), (), 0, shape[axis]) for axis in range(len(shape))]
    result = result.at[tuple(place)].set(smallest)
    longest = shape.index(max(shape))
    place[longest] = (place[longest] + 1) % shape[longest]
    return result.at[tuple(place)].set(largest)


def level_of(stream_key, extent, pieces, least, largest):
    level, own = 1.0, jax.random.fold_in(stream_key, 6)
    for axis_at, parts in pieces:
        heights = jnp.exp(jax.random.uniform(jax.random.fold_in(own, axis_at), (parts,), jnp.float32, least / len(pieces), largest / len(pieces)))
        level = level * jnp.repeat(heights, extent[axis_at] // parts).reshape([-1 if axis == axis_at else 1 for axis in range(len(extent))])
    return level


def normal_values(rng, extent, deviation, limit, pieces=(), kind=jnp.bfloat16):
    values = jax.random.normal(rng, extent, jnp.float32) * deviation
    if len(pieces) > 0:
        values = level_of(rng, extent, pieces, -0.22, 0.18) * values
    return jnp.clip(values, min=-limit, max=limit).astype(kind)


def setup_inputs(seed: int = 0) -> dict:
    keys = jax.random.split(jax.random.key(seed), 6)
    return {
        "images": normal_values(keys[0], (D, IMAGES), 0.03, 0.25, ((0, 32), (1, 32))),
        "texts": normal_values(keys[1], (TEXTS, D), 0.03, 0.25, ((0, 1024),)),
        "positive": set_ends(jax.random.randint(keys[2], (IMAGES,), 0, STEPS * ROWS), jax.random.fold_in(keys[2], 1), 0, (STEPS * ROWS) - 1).astype(jnp.int32),
        "log_scale": jnp.clip(jax.random.uniform(keys[3], (1,), jnp.float32, 2.0, 2.6), 2.0, 2.6),
        "bias": jnp.clip(jax.random.uniform(keys[4], (1,), jnp.float32, -3.0, -1.0), -3.0, -1.0),
    }


EPS = 1e-06

def rounded(value):
    return lax.optimization_barrier(value.astype(jnp.bfloat16)).astype(jnp.float32)

def column_work(args, scale, shift):
    ximg, ytxt, pos = args
    cols = jnp.arange(ROWS, dtype=jnp.int32)
    grad_x = jnp.zeros(ximg.shape, jnp.float32)
    grad_y = jnp.zeros(ytxt.shape, jnp.float32)
    loss = jnp.zeros(pos.shape, jnp.float32)
    for offset in range(STEPS):
        met = jnp.roll(ytxt, offset, axis=0)
        sims = jnp.einsum('dbr,bjd->brj', ximg, met)
        logits = scale * sims + shift
        sign = jnp.where(pos[:, :, None] == offset * ROWS + cols[None, None, :], 1.0, -1.0).astype(jnp.float32)
        loss = loss + lax.optimization_barrier(jnp.sum(jax.nn.softplus(-sign * logits), axis=-1))
        slope = rounded(-sign * jax.nn.sigmoid(-sign * logits))
        grad_x = grad_x + scale * jnp.einsum('brj,bjd->dbr', slope, met)
        piece = scale * jnp.einsum('brj,dbr->bjd', slope, ximg)
        grad_y = grad_y + jnp.roll(piece, -offset, axis=0)
    return (grad_x, grad_y, loss)

def reference(images, texts, positive, log_scale, bias):
    scale = jnp.exp(log_scale[0])
    shift = bias[0]
    img = images.astype(jnp.float32)
    inv_img = lax.rsqrt(lax.optimization_barrier(jnp.sum(img * img, axis=0)) + EPS)
    x32 = img * inv_img[None, :]
    xb = rounded(x32)
    txt = texts.astype(jnp.float32)
    inv_txt = lax.rsqrt(lax.optimization_barrier(jnp.sum(txt * txt, axis=1)) + EPS)
    y32 = txt * inv_txt[:, None]
    yb = rounded(y32)
    ximg = xb.reshape(D, N_BATCH, N_MP, ROWS).transpose(2, 0, 1, 3)
    ytxt = yb.reshape(N_BATCH, N_MP, ROWS, D).transpose(1, 0, 2, 3)
    pos = positive.reshape(N_BATCH, N_MP, ROWS).transpose(1, 0, 2)
    grad_x, grad_y, loss = lax.map(lambda item: column_work(item, scale, shift), (ximg, ytxt, pos))
    grad_x = grad_x.transpose(1, 2, 0, 3).reshape(D, IMAGES)
    grad_y = grad_y.transpose(1, 0, 2, 3).reshape(TEXTS, D)
    loss_rows = loss.transpose(1, 0, 2).reshape(IMAGES) / (STEPS * ROWS)
    image_grad = (inv_img[None, :] * (grad_x - x32 * lax.optimization_barrier(jnp.sum(x32 * grad_x, axis=0))[None, :])).astype(jnp.bfloat16)
    text_grad = inv_txt[:, None] * (grad_y - y32 * lax.optimization_barrier(jnp.sum(y32 * grad_y, axis=1))[:, None])
    return (loss_rows, image_grad, text_grad)
```

```python
import functools

import jax
import jax.numpy as jnp
from jax import lax
from jax.experimental import pallas as pl
from jax.experimental.pallas import tpu as pltpu
from jax.sharding import PartitionSpec as P

STEPS = 4
EPS = 1e-06
LANES = 128
VMEM_BYTES = 24 * 1024 * 1024

TN = (((0,), (0,)), ((), ()))
NT = (((1,), (1,)), ((), ()))
NN = (((1,), (0,)), ((), ()))


def hop(value, steps, parity=None):
    count = lax.axis_size("batch")
    pairs = [(s, (s + steps) % count) for s in range(count) if parity is None or s % 2 == parity]
    return lax.ppermute(value, "batch", pairs)


def swap(value):
    count = lax.axis_size("batch")
    return lax.ppermute(value, "batch", [(s, s ^ 1) for s in range(count)])


def dot(a, b, dims):
    return lax.dot_general(a, b, dims, preferred_element_type=jnp.float32)


def pack_kernel(per, images_ref, out_ref):
    for pair in range(images_ref.shape[1] // (4 * LANES)):
        slabs = []
        for part in range(4):
            at = (4 * pair + part) * LANES
            slabs.append(images_ref[:, at : at + LANES].astype(jnp.float32))
        out_ref[4 * per * pair : 4 * per * (pair + 1), :] = jnp.concatenate(slabs, axis=0).astype(jnp.bfloat16)


def unpack(per, packed_ref, x_ref):
    for pair in range(packed_ref.shape[0] // (4 * per)):
        v = packed_ref[4 * per * pair : 4 * per * (pair + 1), :].astype(jnp.float32)
        for half in range(2):
            low = v[half * per : (half + 1) * per]
            high = v[(2 + half) * per : (3 + half) * per]
            x_ref[2 * per * pair : 2 * per * (pair + 1), half * LANES : (half + 1) * LANES] = jnp.concatenate(
                [low, high], axis=0
            )


def repack(per, x_ref, packed_ref):
    for pair in range(packed_ref.shape[0] // (4 * per)):
        slabs = []
        for part in range(2):
            for half in range(2):
                v = x_ref[2 * per * pair : 2 * per * (pair + 1), half * LANES : (half + 1) * LANES]
                slabs.append(v[part * per : (part + 1) * per])
        packed_ref[4 * per * pair : 4 * per * (pair + 1), :] = jnp.concatenate(slabs, axis=0).astype(jnp.bfloat16)


def inv_rows(block):
    wide = block.astype(jnp.float32)
    return lax.rsqrt(jnp.sum(wide * wide, axis=1, keepdims=True) + EPS)


def inv_cols(wide):
    return lax.rsqrt(jnp.sum(wide * wide, axis=0, keepdims=True) + EPS)


def signs(positive, offset, shape):
    rows = lax.broadcasted_iota(jnp.int32, shape, 0)
    return positive == offset * shape[0] + rows


def spread_kernel(per, packed_ref, out_ref):
    for pair in range(packed_ref.shape[0] // (4 * per)):
        v = packed_ref[4 * per * pair : 4 * per * (pair + 1), :].astype(jnp.float32)
        for part in range(4):
            at = (4 * pair + part) * LANES
            out_ref[:, at : at + LANES] = v[part * per : (part + 1) * per].astype(jnp.bfloat16)


def scale_of(log_scale_ref):
    return jnp.exp(jnp.full((1, 1), log_scale_ref[0], jnp.float32))


def meet(scale, bias, raw, inv_txt, inv_img, hit):
    logits = raw * (scale * inv_txt) * inv_img + bias
    z = jnp.where(hit, -logits, logits)
    small = jnp.exp(-jnp.abs(z))
    sig = jnp.where(z >= 0, 1.0, small) / (1.0 + small)
    return z, small, jnp.where(hit, -sig, sig)


def image_visit(scale, bias, block, xb, inv_img, positive, offset):
    inv_txt = inv_rows(block)
    raw = dot(block, xb, NN)
    z, small, slope = meet(scale, bias, raw, inv_txt, inv_img, signs(positive, offset, raw.shape))
    loss = jnp.sum(jnp.maximum(z, 0.0) + jnp.log1p(small), axis=0, keepdims=True)
    weight = (slope * inv_txt).astype(jnp.bfloat16)
    along = jnp.sum(weight.astype(jnp.float32) * raw, axis=0, keepdims=True)
    return dot(weight, block, TN), loss, along


def early_kernel(
    per, log_scale_ref, bias_ref, packed_ref, own_ref, back2_ref, pos_ref,
    xb_ref, inv_ref, acc_ref, loss_ref, along_ref, x_ref,
):
    scale, bias = scale_of(log_scale_ref), bias_ref[0]
    unpack(per, packed_ref, x_ref)
    x = x_ref[...]
    inv_img = inv_cols(x)
    inv_ref[...] = inv_img
    xb_ref[...] = x.astype(jnp.bfloat16)
    xb = xb_ref[...]
    positive = pos_ref[...]
    part, loss, along = image_visit(scale, bias, own_ref[...], xb, inv_img, positive, 0)
    acc_ref[...] = part
    part, loss2, along2 = image_visit(scale, bias, back2_ref[...], xb, inv_img, positive, 2)
    acc_ref[...] += part
    loss_ref[...] = loss + loss2
    along_ref[...] = along + along2


def late_kernel(
    per, parity_ref, log_scale_ref, bias_ref, xb_ref, inv_ref, early_ref, early_loss_ref, early_along_ref, swap_ref,
    back1_ref, back3_ref, pos_ref, loss_ref, grad_ref, prev_ref, acc_ref, x_ref,
):
    scale, bias = scale_of(log_scale_ref), bias_ref[0]

    @pl.when(parity_ref[0] == 0)
    def _():
        prev_ref[...] = back1_ref[...]

    @pl.when(parity_ref[0] == 1)
    def _():
        prev_ref[...] = swap_ref[...]

    xb, inv_img, positive = xb_ref[...], inv_ref[...], pos_ref[...]
    part, loss, along = image_visit(scale, bias, prev_ref[...], xb, inv_img, positive, 1)
    acc_ref[...] = early_ref[...] + part
    part, loss3, along3 = image_visit(scale, bias, back3_ref[...], xb, inv_img, positive, 3)
    acc_ref[...] += part
    loss_ref[...] = (early_loss_ref[...] + loss + loss3) * (1.0 / (STEPS * prev_ref.shape[0]))
    inner = (early_along_ref[...] + along + along3) * inv_img * inv_img
    x_ref[...] = (scale * inv_img) * (acc_ref[...].T - xb.astype(jnp.float32) * inner)
    repack(per, x_ref, grad_ref)


def text_kernel(
    per, parity_ref, log_scale_ref, bias_ref, own_ref, prev_ref, xb_own_ref, inv_own_ref, img_swap_ref, img_next_ref,
    pos_own_ref, pos_swap_ref, pos_next_ref, send_ref, local_ref, x_ref, xb_ref, acc_ref, pos_ref, inv_ref,
):
    scale, bias = scale_of(log_scale_ref), bias_ref[0]
    odd = parity_ref[0]

    def part(block, inv_txt, xb, inv_img, positive, offset):
        raw = dot(block, xb, NN)
        slope = meet(scale, bias, raw, inv_txt, inv_img, signs(positive, offset, raw.shape))[2]
        return dot((slope * inv_img).astype(jnp.bfloat16), xb, NT)

    prev = prev_ref[...]
    inv_prev = inv_rows(prev)
    acc_ref[...] = part(prev, inv_prev, xb_own_ref[...], inv_own_ref[...], pos_own_ref[...], 1)

    unpack(per, img_swap_ref, x_ref)
    x = x_ref[...]
    acc_ref[...] += part(prev, inv_prev, x.astype(jnp.bfloat16), inv_cols(x), pos_swap_ref[...], 2 - 2 * odd)

    unpack(per, img_next_ref, x_ref)
    x = x_ref[...]
    inv_ref[...] = inv_cols(x)
    xb_ref[...] = x.astype(jnp.bfloat16)
    pos_ref[...] = pos_next_ref[...]
    total = acc_ref[...] + part(prev, inv_prev, xb_ref[...], inv_ref[...], pos_ref[...], 3)
    send_ref[...] = total.astype(jnp.bfloat16)

    @pl.when(odd == 1)
    def _():
        inv_ref[...] = inv_own_ref[...]
        xb_ref[...] = xb_own_ref[...]
        pos_ref[...] = pos_own_ref[...]

    own = own_ref[...]
    local_ref[...] = part(own, inv_rows(own), xb_ref[...], inv_ref[...], pos_ref[...], 2 - 2 * odd)


def finish_kernel(log_scale_ref, own_ref, got_ref, local_ref, out_ref):
    scale = scale_of(log_scale_ref)
    wide = own_ref[...].astype(jnp.float32)
    inv = inv_rows(own_ref[...])
    y = wide * inv
    grad = scale * (got_ref[...].astype(jnp.float32) + local_ref[...])
    out_ref[...] = inv * (grad - y * jnp.sum(y * grad, axis=1, keepdims=True))


SMEM = pl.BlockSpec(memory_space=pltpu.SMEM)
VMEM = pl.BlockSpec(memory_space=pltpu.VMEM)


def call(kernel, out_shape, in_specs, scratch, flops, moved):
    several = isinstance(out_shape, (list, tuple))
    return pl.pallas_call(
        kernel,
        out_shape=out_shape,
        in_specs=in_specs,
        out_specs=tuple(VMEM for _ in out_shape) if several else VMEM,
        scratch_shapes=scratch,
        compiler_params=pltpu.CompilerParams(vmem_limit_bytes=VMEM_BYTES),
        cost_estimate=pl.CostEstimate(flops=flops, bytes_accessed=moved, transcendentals=0),
    )


def shards(images, texts, positive, log_scale, bias):
    per = images.shape[0]
    rows, width = texts.shape
    ranks = lax.axis_size("mp")
    packed_rows = width * rows // LANES
    parity = lax.rem(lax.axis_index("batch"), 2).reshape((1,))
    place = positive.reshape((1, rows))
    flat = jax.ShapeDtypeStruct((packed_rows, LANES), jnp.bfloat16)
    block_bytes = rows * width * 2
    task = 2 * rows * rows * width

    back2 = hop(texts, 2)
    swapped = swap(texts)
    packed = call(functools.partial(pack_kernel, per), flat, [VMEM], [], 0, 2 * block_bytes)(images)
    image = lax.all_to_all(packed, "mp", split_axis=0, concat_axis=0, tiled=True)
    back3 = hop(back2, 1)
    back1 = hop(swapped, 2, 0)
    place_swap = swap(place)
    place_next = hop(place, -2)

    image_next = hop(image, -2)
    image_swap = swap(image)

    square = jax.ShapeDtypeStruct((rows, width), jnp.float32)
    tall = jax.ShapeDtypeStruct((width, rows), jnp.bfloat16)
    line = jax.ShapeDtypeStruct((1, rows), jnp.float32)
    block = jax.ShapeDtypeStruct((rows, width), jnp.bfloat16)
    xb, inv_img, early, early_loss, early_along = call(
        functools.partial(early_kernel, per),
        (tall, line, square, line, line),
        [SMEM] * 2 + [VMEM] * 4,
        [pltpu.VMEM((width, rows), jnp.float32)],
        4 * task,
        6 * block_bytes,
    )(log_scale, bias, image, texts, back2, place)
    loss, grad, prev = call(
        functools.partial(late_kernel, per),
        (line, flat, block),
        [SMEM] * 3 + [VMEM] * 9,
        [pltpu.VMEM((rows, width), jnp.float32), pltpu.VMEM((width, rows), jnp.float32)],
        4 * task,
        7 * block_bytes,
    )(parity, log_scale, bias, xb, inv_img, early, early_loss, early_along, swapped, back1, back3, place)
    image_grad = lax.all_to_all(grad, "mp", split_axis=0, concat_axis=0, tiled=True)

    send, local = call(
        functools.partial(text_kernel, per),
        (block, square),
        [SMEM] * 3 + [VMEM] * 9,
        [
            pltpu.VMEM((width, rows), jnp.float32),
            pltpu.VMEM((width, rows), jnp.bfloat16),
            pltpu.VMEM((rows, width), jnp.float32),
            pltpu.VMEM((1, rows), jnp.int32),
            pltpu.VMEM((1, rows), jnp.float32),
        ],
        8 * task,
        9 * block_bytes,
    )(parity, log_scale, bias, texts, prev, xb, inv_img, image_swap, image_next, place, place_swap, place_next)
    got = hop(send, -1)
    text_grad = call(finish_kernel, square, [SMEM] + [VMEM] * 3, [], 0, 6 * block_bytes)(log_scale, texts, got, local)

    wide = jax.ShapeDtypeStruct((per, ranks * rows), jnp.bfloat16)
    image_grad = call(functools.partial(spread_kernel, per), wide, [VMEM], [], 0, 2 * block_bytes)(image_grad)
    return (loss.reshape((rows,)), image_grad, text_grad)


def solution(mesh):
    in_specs = (P("mp", "batch"), P(("batch", "mp"), None), P(("batch", "mp")), P(), P())
    out_specs = (P(("batch", "mp")), P("mp", "batch"), P(("batch", "mp"), None))
    return jax.shard_map(shards, mesh=mesh, in_specs=in_specs, out_specs=out_specs, check_vma=False)
```

```python
import functools

import jax
import jax.numpy as jnp
from jax import lax
from jax.experimental import pallas as pl
from jax.experimental.pallas import tpu as pltpu
from jax.sharding import PartitionSpec as P

STEPS = 4
EPS = 1e-06
LANES = 128
TAIL = 16
PARTS = 4
VMEM_BYTES = 24 * 1024 * 1024

TN = (((0,), (0,)), ((), ()))
NT = (((1,), (1,)), ((), ()))
NN = (((1,), (0,)), ((), ()))


def hop(value, steps, parity=None):
    count = lax.axis_size("batch")
    pairs = [(s, (s + steps) % count) for s in range(count) if parity is None or s % 2 == parity]
    return lax.ppermute(value, "batch", pairs)


def swap(value):
    count = lax.axis_size("batch")
    return lax.ppermute(value, "batch", [(s, s ^ 1) for s in range(count)])


def dot(a, b, dims):
    return lax.dot_general(a, b, dims, preferred_element_type=jnp.float32)


def pack_kernel(per, images_ref, out_ref, in_ref, packed_ref, in_sem, out_sem):
    parts = in_sem.shape[0]
    columns = images_ref.shape[1] // parts
    lines = out_ref.shape[0] // parts

    def load(i):
        at = pl.ds(columns * i, columns)
        return pltpu.make_async_copy(images_ref.at[:, at], in_ref.at[:, at], in_sem.at[i])

    def store(i):
        at = pl.ds(lines * i, lines)
        return pltpu.make_async_copy(packed_ref.at[at], out_ref.at[at], out_sem.at[i])

    for i in range(parts):
        load(i).start()
    for i in range(parts):
        load(i).wait()
        for pair in range(columns * i // (4 * LANES), columns * (i + 1) // (4 * LANES)):
            slabs = []
            for part in range(4):
                at = (4 * pair + part) * LANES
                slabs.append(in_ref[:, at : at + LANES].astype(jnp.float32))
            packed_ref[4 * per * pair : 4 * per * (pair + 1), :] = jnp.concatenate(slabs, axis=0).astype(jnp.bfloat16)
        store(i).start()
    for i in range(parts):
        store(i).wait()


def gather_kernel(per, packed_ref, pos_ref, out_ref):
    width = packed_ref.shape[0] // 2
    for group in range(width // (4 * per)):
        v = packed_ref[8 * per * group : 8 * per * (group + 1), :].astype(jnp.float32)
        for half in range(2):
            slabs = [v[(2 * part + half) * per : (2 * part + half + 1) * per] for part in range(4)]
            out_ref[4 * per * group : 4 * per * (group + 1), half * LANES : (half + 1) * LANES] = jnp.concatenate(
                slabs, axis=0
            ).astype(jnp.bfloat16)
    positive = pos_ref[...]
    count = positive.shape[1]
    step = jnp.floor(positive.astype(jnp.float32) * (1.0 / count))
    row = positive.astype(jnp.float32) - step * count
    lines = lax.broadcasted_iota(jnp.int32, (TAIL, count), 0)
    out_ref[width:, :] = jnp.where(lines == 0, step, jnp.where(lines == 1, row, 0.0)).astype(jnp.bfloat16)


def repack(per, x_ref, packed_ref):
    for pair in range(packed_ref.shape[0] // (4 * per)):
        slabs = []
        for part in range(2):
            for half in range(2):
                v = x_ref[2 * per * pair : 2 * per * (pair + 1), half * LANES : (half + 1) * LANES]
                slabs.append(v[part * per : (part + 1) * per])
        packed_ref[4 * per * pair : 4 * per * (pair + 1), :] = jnp.concatenate(slabs, axis=0).astype(jnp.bfloat16)


def spread_kernel(per, packed_ref, out_ref):
    for pair in range(packed_ref.shape[0] // (4 * per)):
        v = packed_ref[4 * per * pair : 4 * per * (pair + 1), :].astype(jnp.float32)
        for part in range(4):
            at = (4 * pair + part) * LANES
            out_ref[:, at : at + LANES] = v[part * per : (part + 1) * per].astype(jnp.bfloat16)


def inv_rows(block):
    wide = block.astype(jnp.float32)
    return lax.rsqrt(jnp.sum(wide * wide, axis=1, keepdims=True) + EPS)


def inv_cols(block):
    wide = block.astype(jnp.float32)
    return lax.rsqrt(jnp.sum(wide * wide, axis=0, keepdims=True) + EPS)


def read_images(ref):
    width = ref.shape[0] - TAIL
    tail = ref[width:, :].astype(jnp.float32)
    positive = (tail[0:1] * ref.shape[1] + tail[1:2]).astype(jnp.int32)
    xb = ref[:width, :]
    return xb, inv_cols(xb), positive


def signs(positive, offset, shape):
    rows = lax.broadcasted_iota(jnp.int32, shape, 0)
    return positive == offset * shape[0] + rows


def scale_of(log_scale_ref):
    return jnp.exp(jnp.full((1, 1), log_scale_ref[0], jnp.float32))


def meet(scale, bias, raw, inv_txt, inv_img, hit):
    logits = raw * (scale * inv_txt) * inv_img + bias
    growth = jnp.exp(jnp.where(hit, -logits, logits))
    sig = growth / (1.0 + growth)
    return growth, jnp.where(hit, -sig, sig)


def softplus_sum(growth):
    parts = jnp.split(growth, 4, axis=0)
    while len(parts) > 1:
        parts = [a + b + a * b for a, b in zip(parts[::2], parts[1::2])]
    return jnp.sum(jnp.log1p(parts[0]), axis=0, keepdims=True)


def image_visit(scale, bias, block, xb, inv_img, positive, offset, inv_txt):
    raw = dot(block, xb, NN)
    growth, slope = meet(scale, bias, raw, inv_txt, inv_img, signs(positive, offset, raw.shape))
    weight = (slope * inv_txt).astype(jnp.bfloat16)
    along = jnp.sum(weight.astype(jnp.float32) * raw, axis=0, keepdims=True)
    return dot(weight, block, TN), softplus_sum(growth), along


def norm_kernel(own_ref, back2_ref, inv_own_ref, inv_back2_ref, copy_ref):
    inv_own_ref[...] = inv_rows(own_ref[...])
    inv_back2_ref[...] = inv_rows(back2_ref[...])
    copy_ref[...] = back2_ref[...]


def early_kernel(log_scale_ref, bias_ref, image_ref, own_ref, back2_ref, inv_own_ref, inv_back2_ref, acc_ref, loss_ref, along_ref):
    scale, bias = scale_of(log_scale_ref), bias_ref[0]
    xb, inv_img, positive = read_images(image_ref)
    part, loss, along = image_visit(scale, bias, own_ref[...], xb, inv_img, positive, 0, inv_own_ref[...])
    acc_ref[...] = part
    part, loss2, along2 = image_visit(scale, bias, back2_ref[...], xb, inv_img, positive, 2, inv_back2_ref[...])
    acc_ref[...] += part
    loss_ref[...] = loss + loss2
    along_ref[...] = along + along2


def pick(odd, when_odd_ref, when_even_ref):
    return jnp.where(odd == 1, when_odd_ref[...], when_even_ref[...])


def late_kernel(
    per, parity_ref, log_scale_ref, bias_ref, image_ref, early_ref, early_loss_ref, early_along_ref, swap_ref,
    back1_ref, back3_ref, loss_ref, grad_ref, acc_ref, x_ref,
):
    scale, bias = scale_of(log_scale_ref), bias_ref[0]
    xb, inv_img, positive = read_images(image_ref)
    prev = pick(parity_ref[0], swap_ref, back1_ref)
    part, loss, along = image_visit(scale, bias, prev, xb, inv_img, positive, 1, inv_rows(prev))
    acc_ref[...] = early_ref[...] + part
    back3 = back3_ref[...]
    part, loss3, along3 = image_visit(scale, bias, back3, xb, inv_img, positive, 3, inv_rows(back3))
    acc_ref[...] += part
    loss_ref[...] = (early_loss_ref[...] + loss + loss3) * (1.0 / (STEPS * back3_ref.shape[0]))
    inner = (early_along_ref[...] + along + along3) * inv_img * inv_img
    x_ref[...] = (scale * inv_img) * (acc_ref[...].T - xb.astype(jnp.float32) * inner)
    repack(per, x_ref, grad_ref)


def text_visit(scale, bias, block, inv_txt, images, offset):
    xb, inv_img, positive = images
    raw = dot(block, xb, NN)
    slope = meet(scale, bias, raw, inv_txt, inv_img, signs(positive, offset, raw.shape))[1]
    return dot((slope * inv_img).astype(jnp.bfloat16), xb, NT)


def text_own_kernel(
    parity_ref, log_scale_ref, bias_ref, swap_ref, back1_ref, image_ref, after_ref, acc_ref, inv_ref, prev_ref
):
    scale, bias = scale_of(log_scale_ref), bias_ref[0]
    prev = pick(parity_ref[0], swap_ref, back1_ref)
    prev_ref[...] = prev
    inv_prev = inv_rows(prev)
    inv_ref[...] = inv_prev
    acc_ref[...] = text_visit(scale, bias, prev, inv_prev, read_images(image_ref), 1)


def text_send_kernel(
    parity_ref, log_scale_ref, bias_ref, prev_ref, inv_ref, acc_ref, img_swap_ref, img_next_ref, send_ref, sum_ref
):
    scale, bias = scale_of(log_scale_ref), bias_ref[0]
    prev, inv_prev = prev_ref[...], inv_ref[...]
    offset = 2 - 2 * parity_ref[0]
    sum_ref[...] = acc_ref[...] + text_visit(scale, bias, prev, inv_prev, read_images(img_next_ref), 3)
    total = sum_ref[...] + text_visit(scale, bias, prev, inv_prev, read_images(img_swap_ref), offset)
    send_ref[...] = total.astype(jnp.bfloat16)


def text_local_kernel(
    parity_ref, log_scale_ref, bias_ref, own_ref, image_ref, img_next_ref, after_ref, local_ref, pick_ref
):
    scale, bias = scale_of(log_scale_ref), bias_ref[0]
    odd = parity_ref[0]
    pick_ref[...] = pick(odd, image_ref, img_next_ref)
    own = own_ref[...]
    local_ref[...] = text_visit(scale, bias, own, inv_rows(own), read_images(pick_ref), 2 - 2 * odd)


def finish_kernel(log_scale_ref, own_ref, got_ref, local_ref, out_ref, in_ref, grad_ref, in_sem, out_sem):
    scale = scale_of(log_scale_ref)
    parts = in_sem.shape[0]
    rows = out_ref.shape[0] // parts

    def load(i):
        at = pl.ds(rows * i, rows)
        return pltpu.make_async_copy(got_ref.at[at], in_ref.at[at], in_sem.at[i])

    def store(i):
        at = pl.ds(rows * i, rows)
        return pltpu.make_async_copy(grad_ref.at[at], out_ref.at[at], out_sem.at[i])

    for i in range(parts):
        load(i).start()
    for i in range(parts):
        at = pl.ds(rows * i, rows)
        own = own_ref[at]
        inv = inv_rows(own)
        y = own.astype(jnp.float32) * inv
        load(i).wait()
        grad = scale * (in_ref[at].astype(jnp.float32) + local_ref[at])
        grad_ref[at] = inv * (grad - y * jnp.sum(y * grad, axis=1, keepdims=True))
        store(i).start()
    for i in range(parts):
        store(i).wait()


HBM = pl.BlockSpec(memory_space=pltpu.HBM)
SMEM = pl.BlockSpec(memory_space=pltpu.SMEM)
VMEM = pl.BlockSpec(memory_space=pltpu.VMEM)


def call(kernel, out_shape, in_specs, scratch, flops, moved, out_spec=None, limit=VMEM_BYTES):
    several = isinstance(out_shape, (list, tuple))
    return pl.pallas_call(
        kernel,
        out_shape=out_shape,
        in_specs=in_specs,
        out_specs=tuple(VMEM for _ in out_shape) if several else out_spec or VMEM,
        scratch_shapes=scratch,
        compiler_params=pltpu.CompilerParams(vmem_limit_bytes=limit),
        cost_estimate=pl.CostEstimate(flops=flops, bytes_accessed=moved, transcendentals=0),
    )


def shards(images, texts, positive, log_scale, bias):
    per = images.shape[0]
    rows, width = texts.shape
    ranks = lax.axis_size("mp")
    packed_rows = width * rows // LANES
    parity = lax.rem(lax.axis_index("batch"), 2).reshape((1,))
    place = positive.reshape((1, rows))
    flat = jax.ShapeDtypeStruct((packed_rows, LANES), jnp.bfloat16)
    block_bytes = rows * width * 2
    task = 2 * rows * rows * width

    square = jax.ShapeDtypeStruct((rows, width), jnp.float32)
    line = jax.ShapeDtypeStruct((1, rows), jnp.float32)
    block = jax.ShapeDtypeStruct((rows, width), jnp.bfloat16)
    tall = jax.ShapeDtypeStruct((width + TAIL, rows), jnp.bfloat16)
    scalars = (parity, log_scale, bias)

    back2 = hop(texts, 2)
    swapped = swap(texts)
    packed = call(functools.partial(pack_kernel, per), flat, [HBM], [
            pltpu.VMEM(images.shape, jnp.bfloat16),
            pltpu.VMEM(flat.shape, jnp.bfloat16),
            pltpu.SemaphoreType.DMA((PARTS,)),
            pltpu.SemaphoreType.DMA((PARTS,)),
        ], 0, 2 * block_bytes, HBM, 60 * 1024 * 1024)(images)
    back3 = hop(back2, 1)
    back1 = hop(swapped, 2, 0)

    packed = lax.all_to_all(packed, "mp", split_axis=0, concat_axis=0, tiled=True)
    image = call(functools.partial(gather_kernel, per), tall, [VMEM] * 2, [], 0, 2 * block_bytes)(packed, place)
    image_swap = swap(image)
    image_next = hop(image, -2)

    column = jax.ShapeDtypeStruct((rows, 1), jnp.float32)
    inv_own, inv_back2, near2 = call(norm_kernel, (column, column, block), [VMEM] * 2, [], 10_000_000_000, 2 * block_bytes)(texts, back2)
    early, early_loss, early_along = call(
        early_kernel, (square, line, line), [SMEM] * 2 + [VMEM] * 5, [], 4 * task, 5 * block_bytes
    )(log_scale, bias, image, texts, near2, inv_own, inv_back2)
    loss, grad = call(
        functools.partial(late_kernel, per),
        (line, flat),
        [SMEM] * 3 + [VMEM] * 7,
        [pltpu.VMEM((rows, width), jnp.float32), pltpu.VMEM((width, rows), jnp.float32)],
        4 * task,
        7 * block_bytes,
    )(*scalars, image, early, early_loss, early_along, swapped, back1, back3)
    image_grad = lax.all_to_all(grad, "mp", split_axis=0, concat_axis=0, tiled=True)

    text_own, inv_prev, prev = call(
        text_own_kernel, (square, column, block), [SMEM] * 3 + [VMEM] * 4, [], 2 * task, 4 * block_bytes
    )(*scalars, swapped, back1, image, loss)
    send = call(
        text_send_kernel, block, [SMEM] * 3 + [VMEM] * 5, [pltpu.VMEM((rows, width), jnp.float32)], 4 * task, 6 * block_bytes
    )(*scalars, prev, inv_prev, text_own, image_swap, image_next)
    got = hop(send, -1)
    local = call(
        text_local_kernel,
        square,
        [SMEM] * 3 + [VMEM] * 4,
        [pltpu.VMEM((width + TAIL, rows), jnp.bfloat16)],
        2 * task,
        5 * block_bytes,
    )(*scalars, texts, image, image_next, send)
    text_grad = call(
        finish_kernel,
        square,
        [SMEM, VMEM, HBM, VMEM],
        [
            pltpu.VMEM((rows, width), jnp.bfloat16),
            pltpu.VMEM((rows, width), jnp.float32),
            pltpu.SemaphoreType.DMA((PARTS,)),
            pltpu.SemaphoreType.DMA((PARTS,)),
        ],
        0,
        6 * block_bytes,
        HBM,
    )(log_scale, texts, got, local)

    wide = jax.ShapeDtypeStruct((per, ranks * rows), jnp.bfloat16)
    image_grad = call(functools.partial(spread_kernel, per), wide, [VMEM], [], 0, 2 * block_bytes)(image_grad)
    return (loss.reshape((rows,)), image_grad, text_grad)


def solution(mesh):
    in_specs = (P("mp", "batch"), P(("batch", "mp"), None), P(("batch", "mp")), P(), P())
    out_specs = (P(("batch", "mp")), P("mp", "batch"), P(("batch", "mp"), None))
    return jax.shard_map(shards, mesh=mesh, in_specs=in_specs, out_specs=out_specs, check_vma=False)
```

```python
import functools

import jax
import jax.numpy as jnp
from jax import lax
from jax.experimental import pallas as pl
from jax.experimental.pallas import tpu as pltpu
from jax.sharding import PartitionSpec as P

STEPS = 4
EPS = 1e-06
LANES = 128
TAIL = 16
PARTS = 4
VMEM_BYTES = 24 * 1024 * 1024

TN = (((0,), (0,)), ((), ()))
NT = (((1,), (1,)), ((), ()))
NN = (((1,), (0,)), ((), ()))


def hop(value, steps, parity=None):
    count = lax.axis_size("batch")
    pairs = [(s, (s + steps) % count) for s in range(count) if parity is None or s % 2 == parity]
    return lax.ppermute(value, "batch", pairs)


def swap(value):
    count = lax.axis_size("batch")
    return lax.ppermute(value, "batch", [(s, s ^ 1) for s in range(count)])


def dot(a, b, dims):
    return lax.dot_general(a, b, dims, preferred_element_type=jnp.float32)


def pack_kernel(per, images_ref, out_ref, in_ref, packed_ref, in_sem, out_sem):
    parts = in_sem.shape[0]
    columns = images_ref.shape[1] // parts
    lines = out_ref.shape[0] // parts

    def load(i):
        at = pl.ds(columns * i, columns)
        return pltpu.make_async_copy(images_ref.at[:, at], in_ref.at[:, at], in_sem.at[i])

    def store(i):
        at = pl.ds(lines * i, lines)
        return pltpu.make_async_copy(packed_ref.at[at], out_ref.at[at], out_sem.at[i])

    for i in range(parts):
        load(i).start()
    for i in range(parts):
        load(i).wait()
        for pair in range(columns * i // (4 * LANES), columns * (i + 1) // (4 * LANES)):
            slabs = []
            for part in range(4):
                at = (4 * pair + part) * LANES
                slabs.append(in_ref[:, at : at + LANES].astype(jnp.float32))
            packed_ref[4 * per * pair : 4 * per * (pair + 1), :] = jnp.concatenate(slabs, axis=0).astype(jnp.bfloat16)
        store(i).start()
    for i in range(parts):
        store(i).wait()


def gather_kernel(per, packed_ref, pos_ref, after_ref, out_ref):
    width = packed_ref.shape[0] // 2
    for group in range(width // (4 * per)):
        v = packed_ref[8 * per * group : 8 * per * (group + 1), :].astype(jnp.float32)
        for half in range(2):
            slabs = [v[(2 * part + half) * per : (2 * part + half + 1) * per] for part in range(4)]
            out_ref[4 * per * group : 4 * per * (group + 1), half * LANES : (half + 1) * LANES] = jnp.concatenate(
                slabs, axis=0
            ).astype(jnp.bfloat16)
    positive = pos_ref[...]
    count = positive.shape[1]
    step = jnp.floor(positive.astype(jnp.float32) * (1.0 / count))
    row = positive.astype(jnp.float32) - step * count
    lines = lax.broadcasted_iota(jnp.int32, (TAIL, count), 0)
    out_ref[width:, :] = jnp.where(lines == 0, step, jnp.where(lines == 1, row, 0.0)).astype(jnp.bfloat16)


def repack(per, x_ref, packed_ref):
    for pair in range(packed_ref.shape[0] // (4 * per)):
        slabs = []
        for part in range(2):
            for half in range(2):
                v = x_ref[2 * per * pair : 2 * per * (pair + 1), half * LANES : (half + 1) * LANES]
                slabs.append(v[part * per : (part + 1) * per])
        packed_ref[4 * per * pair : 4 * per * (pair + 1), :] = jnp.concatenate(slabs, axis=0).astype(jnp.bfloat16)


def spread_kernel(per, packed_ref, out_ref):
    for pair in range(packed_ref.shape[0] // (4 * per)):
        v = packed_ref[4 * per * pair : 4 * per * (pair + 1), :].astype(jnp.float32)
        for part in range(4):
            at = (4 * pair + part) * LANES
            out_ref[:, at : at + LANES] = v[part * per : (part + 1) * per].astype(jnp.bfloat16)


def inv_rows(block):
    wide = block.astype(jnp.float32)
    return lax.rsqrt(jnp.sum(wide * wide, axis=1, keepdims=True) + EPS)


def inv_cols(block):
    wide = block.astype(jnp.float32)
    return lax.rsqrt(jnp.sum(wide * wide, axis=0, keepdims=True) + EPS)


def read_images(ref):
    width = ref.shape[0] - TAIL
    tail = ref[width:, :].astype(jnp.float32)
    positive = (tail[0:1] * ref.shape[1] + tail[1:2]).astype(jnp.int32)
    xb = ref[:width, :]
    return xb, inv_cols(xb), positive


def signs(positive, offset, shape):
    rows = lax.broadcasted_iota(jnp.int32, shape, 0)
    return positive == offset * shape[0] + rows


def scale_of(log_scale_ref):
    return jnp.exp(jnp.full((1, 1), log_scale_ref[0], jnp.float32))


def meet(scale, bias, raw, inv_txt, inv_img, hit):
    logits = raw * (scale * inv_txt) * inv_img + bias
    growth = jnp.exp(jnp.where(hit, -logits, logits))
    sig = growth / (1.0 + growth)
    return growth, jnp.where(hit, -sig, sig)


def softplus_sum(growth):
    parts = jnp.split(growth, 4, axis=0)
    while len(parts) > 1:
        parts = [a + b + a * b for a, b in zip(parts[::2], parts[1::2])]
    return jnp.sum(jnp.log1p(parts[0]), axis=0, keepdims=True)


def image_visit(scale, bias, block, xb, inv_img, positive, offset, inv_txt):
    raw = dot(block, xb, NN)
    growth, slope = meet(scale, bias, raw, inv_txt, inv_img, signs(positive, offset, raw.shape))
    weight = (slope * inv_txt).astype(jnp.bfloat16)
    along = jnp.sum(weight.astype(jnp.float32) * raw, axis=0, keepdims=True)
    return dot(weight, block, TN), softplus_sum(growth), along


def arrived_kernel(back2_ref, out_ref):
    out_ref[...] = jnp.zeros(out_ref.shape, jnp.float32)


def fetch(source_ref, target_ref, sem):
    return pltpu.make_async_copy(source_ref, target_ref, sem)


def early_kernel(
    log_scale_ref, bias_ref, image_ref, own_ref, back2_ref, acc_ref, loss_ref, along_ref, near_ref, sem
):
    load = fetch(back2_ref, near_ref, sem)
    load.start()
    scale, bias = scale_of(log_scale_ref), bias_ref[0]
    xb, inv_img, positive = read_images(image_ref)
    own = own_ref[...]
    part, loss, along = image_visit(scale, bias, own, xb, inv_img, positive, 0, inv_rows(own))
    acc_ref[...] = part
    load.wait()
    back2 = near_ref[...]
    part, loss2, along2 = image_visit(scale, bias, back2, xb, inv_img, positive, 2, inv_rows(back2))
    acc_ref[...] += part
    loss_ref[...] = loss + loss2
    along_ref[...] = along + along2


def pick(odd, when_odd_ref, when_even_ref):
    return jnp.where(odd == 1, when_odd_ref[...], when_even_ref[...])


def late_kernel(
    per, parity_ref, log_scale_ref, bias_ref, image_ref, early_ref, early_loss_ref, early_along_ref, swap_ref,
    back1_ref, back3_ref, loss_ref, grad_ref, acc_ref, x_ref, near_ref, sem,
):
    load = fetch(back3_ref, near_ref, sem)
    load.start()
    scale, bias = scale_of(log_scale_ref), bias_ref[0]
    xb, inv_img, positive = read_images(image_ref)
    prev = pick(parity_ref[0], swap_ref, back1_ref)
    part, loss, along = image_visit(scale, bias, prev, xb, inv_img, positive, 1, inv_rows(prev))
    acc_ref[...] = early_ref[...] + part
    load.wait()
    back3 = near_ref[...]
    part, loss3, along3 = image_visit(scale, bias, back3, xb, inv_img, positive, 3, inv_rows(back3))
    acc_ref[...] += part
    loss_ref[...] = (early_loss_ref[...] + loss + loss3) * (1.0 / (STEPS * back3_ref.shape[0]))
    inner = (early_along_ref[...] + along + along3) * inv_img * inv_img
    x_ref[...] = (scale * inv_img) * (acc_ref[...].T - xb.astype(jnp.float32) * inner)
    repack(per, x_ref, grad_ref)


def text_visit(scale, bias, block, inv_txt, images, offset):
    xb, inv_img, positive = images
    raw = dot(block, xb, NN)
    slope = meet(scale, bias, raw, inv_txt, inv_img, signs(positive, offset, raw.shape))[1]
    return dot((slope * inv_img).astype(jnp.bfloat16), xb, NT)


def text_own_kernel(
    parity_ref, log_scale_ref, bias_ref, swap_ref, back1_ref, image_ref, after_ref, acc_ref, inv_ref, prev_ref
):
    scale, bias = scale_of(log_scale_ref), bias_ref[0]
    prev = pick(parity_ref[0], swap_ref, back1_ref)
    prev_ref[...] = prev
    inv_prev = inv_rows(prev)
    inv_ref[...] = inv_prev
    acc_ref[...] = text_visit(scale, bias, prev, inv_prev, read_images(image_ref), 1)


def text_send_kernel(log_scale_ref, bias_ref, prev_ref, inv_ref, acc_ref, img_next_ref, send_ref):
    scale, bias = scale_of(log_scale_ref), bias_ref[0]
    total = acc_ref[...] + text_visit(scale, bias, prev_ref[...], inv_ref[...], read_images(img_next_ref), 3)
    send_ref[...] = total.astype(jnp.bfloat16)


def text_local_kernel(log_scale_ref, bias_ref, own_ref, image_ref, img_next_ref, after_ref, local_ref):
    scale, bias = scale_of(log_scale_ref), bias_ref[0]
    own = own_ref[...]
    inv_own = inv_rows(own)
    local_ref[...] = text_visit(scale, bias, own, inv_own, read_images(image_ref), 0)
    local_ref[...] += text_visit(scale, bias, own, inv_own, read_images(img_next_ref), 2)


def finish_kernel(log_scale_ref, own_ref, got_ref, local_ref, out_ref, grad_ref, out_sem):
    scale = scale_of(log_scale_ref)
    parts = out_sem.shape[0]
    rows = out_ref.shape[0] // parts

    def store(i):
        at = pl.ds(rows * i, rows)
        return pltpu.make_async_copy(grad_ref.at[at], out_ref.at[at], out_sem.at[i])

    for i in range(parts):
        at = pl.ds(rows * i, rows)
        own = own_ref[at]
        inv = inv_rows(own)
        y = own.astype(jnp.float32) * inv
        grad = scale * (got_ref[at].astype(jnp.float32) + local_ref[at])
        grad_ref[at] = inv * (grad - y * jnp.sum(y * grad, axis=1, keepdims=True))
        store(i).start()
    for i in range(parts):
        store(i).wait()


HBM = pl.BlockSpec(memory_space=pltpu.HBM)
SMEM = pl.BlockSpec(memory_space=pltpu.SMEM)
VMEM = pl.BlockSpec(memory_space=pltpu.VMEM)


def call(kernel, out_shape, in_specs, scratch, flops, moved, out_spec=None, limit=VMEM_BYTES):
    several = isinstance(out_shape, (list, tuple))
    return pl.pallas_call(
        kernel,
        out_shape=out_shape,
        in_specs=in_specs,
        out_specs=tuple(VMEM for _ in out_shape) if several else out_spec or VMEM,
        scratch_shapes=scratch,
        compiler_params=pltpu.CompilerParams(vmem_limit_bytes=limit),
        cost_estimate=pl.CostEstimate(flops=flops, bytes_accessed=moved, transcendentals=0),
    )


def shards(images, texts, positive, log_scale, bias):
    per = images.shape[0]
    rows, width = texts.shape
    ranks = lax.axis_size("mp")
    packed_rows = width * rows // LANES
    parity = lax.rem(lax.axis_index("batch"), 2).reshape((1,))
    place = positive.reshape((1, rows))
    flat = jax.ShapeDtypeStruct((packed_rows, LANES), jnp.bfloat16)
    block_bytes = rows * width * 2
    task = 2 * rows * rows * width

    square = jax.ShapeDtypeStruct((rows, width), jnp.float32)
    line = jax.ShapeDtypeStruct((1, rows), jnp.float32)
    block = jax.ShapeDtypeStruct((rows, width), jnp.bfloat16)
    tall = jax.ShapeDtypeStruct((width + TAIL, rows), jnp.bfloat16)
    scalars = (parity, log_scale, bias)

    back2 = hop(texts, 2)
    swapped = swap(texts)
    packed = call(functools.partial(pack_kernel, per), flat, [HBM], [
            pltpu.VMEM(images.shape, jnp.bfloat16),
            pltpu.VMEM(flat.shape, jnp.bfloat16),
            pltpu.SemaphoreType.DMA((PARTS,)),
            pltpu.SemaphoreType.DMA((PARTS,)),
        ], 0, 2 * block_bytes, HBM, 60 * 1024 * 1024)(images)
    back3 = hop(back2, 1)
    back1 = hop(swapped, 2, 0)

    packed = lax.all_to_all(packed, "mp", split_axis=0, concat_axis=0, tiled=True)
    column = jax.ShapeDtypeStruct((rows, 1), jnp.float32)
    tile = jax.ShapeDtypeStruct((8, LANES), jnp.float32)
    arrived = call(arrived_kernel, tile, [HBM], [], 10_000_000_000, block_bytes)(back2)
    image = call(functools.partial(gather_kernel, per), tall, [VMEM] * 3, [], 0, 2 * block_bytes)(
        packed, place, arrived
    )
    image_next = hop(image, -2)

    near_block = [pltpu.VMEM((rows, width), jnp.bfloat16), pltpu.SemaphoreType.DMA]
    early, early_loss, early_along = call(
        early_kernel, (square, line, line), [SMEM] * 2 + [VMEM] * 2 + [HBM], near_block, 4 * task, 5 * block_bytes
    )(log_scale, bias, image, texts, back2)
    loss, grad = call(
        functools.partial(late_kernel, per),
        (line, flat),
        [SMEM] * 3 + [VMEM] * 6 + [HBM],
        [pltpu.VMEM((rows, width), jnp.float32), pltpu.VMEM((width, rows), jnp.float32)] + near_block,
        4 * task,
        7 * block_bytes,
    )(*scalars, image, early, early_loss, early_along, swapped, back1, back3)
    image_grad = lax.all_to_all(grad, "mp", split_axis=0, concat_axis=0, tiled=True)

    text_own, inv_prev, prev = call(
        text_own_kernel, (square, column, block), [SMEM] * 3 + [VMEM] * 4, [], 2 * task, 4 * block_bytes
    )(*scalars, swapped, back1, image, loss)
    send = call(text_send_kernel, block, [SMEM] * 2 + [VMEM] * 4, [], 2 * task, 5 * block_bytes)(
        log_scale, bias, prev, inv_prev, text_own, image_next
    )
    got = hop(send, -1)
    local = call(text_local_kernel, square, [SMEM] * 2 + [VMEM] * 4, [], 4 * task, 5 * block_bytes)(
        log_scale, bias, texts, image, image_next, send
    )
    text_grad = call(
        finish_kernel,
        square,
        [SMEM, VMEM, VMEM, VMEM],
        [
            pltpu.VMEM((rows, width), jnp.float32),
            pltpu.SemaphoreType.DMA((PARTS,)),
        ],
        0,
        6 * block_bytes,
        HBM,
    )(log_scale, texts, got, local)

    wide = jax.ShapeDtypeStruct((per, ranks * rows), jnp.bfloat16)
    image_grad = call(functools.partial(spread_kernel, per), wide, [VMEM], [], 0, 2 * block_bytes)(image_grad)
    return (loss.reshape((rows,)), image_grad, text_grad)


def solution(mesh):
    in_specs = (P("mp", "batch"), P(("batch", "mp"), None), P(("batch", "mp")), P(), P())
    out_specs = (P(("batch", "mp")), P("mp", "batch"), P(("batch", "mp"), None))
    return jax.shard_map(shards, mesh=mesh, in_specs=in_specs, out_specs=out_specs, check_vma=False)
```

```python
import functools

import jax
import jax.numpy as jnp
from jax import lax
from jax.experimental import pallas as pl
from jax.experimental.pallas import tpu as pltpu
from jax.sharding import PartitionSpec as P

STEPS = 4
EPS = 1e-06
LANES = 128
TAIL = 16
PARTS = 4
VMEM_BYTES = 24 * 1024 * 1024

TN = (((0,), (0,)), ((), ()))
NT = (((1,), (1,)), ((), ()))
NN = (((1,), (0,)), ((), ()))


def hop(value, steps, parity=None):
    count = lax.axis_size("batch")
    pairs = [(s, (s + steps) % count) for s in range(count) if parity is None or s % 2 == parity]
    return lax.ppermute(value, "batch", pairs)


def swap(value):
    count = lax.axis_size("batch")
    return lax.ppermute(value, "batch", [(s, s ^ 1) for s in range(count)])


def dot(a, b, dims):
    return lax.dot_general(a, b, dims, preferred_element_type=jnp.float32)


def pack_kernel(per, images_ref, out_ref, in_ref, packed_ref, in_sem, out_sem):
    parts = in_sem.shape[0]
    columns = images_ref.shape[1] // parts
    lines = out_ref.shape[0] // parts

    def load(i):
        at = pl.ds(columns * i, columns)
        return pltpu.make_async_copy(images_ref.at[:, at], in_ref.at[:, at], in_sem.at[i])

    def store(i):
        at = pl.ds(lines * i, lines)
        return pltpu.make_async_copy(packed_ref.at[at], out_ref.at[at], out_sem.at[i])

    for i in range(parts):
        load(i).start()
    for i in range(parts):
        load(i).wait()
        for pair in range(columns * i // (4 * LANES), columns * (i + 1) // (4 * LANES)):
            slabs = []
            for part in range(4):
                at = (4 * pair + part) * LANES
                slabs.append(in_ref[:, at : at + LANES].astype(jnp.float32))
            packed_ref[4 * per * pair : 4 * per * (pair + 1), :] = jnp.concatenate(slabs, axis=0).astype(jnp.bfloat16)
        store(i).start()
    for i in range(parts):
        store(i).wait()


def gather_kernel(per, packed_ref, pos_ref, after_ref, out_ref):
    width = packed_ref.shape[0] // 2
    for group in range(width // (4 * per)):
        v = packed_ref[8 * per * group : 8 * per * (group + 1), :].astype(jnp.float32)
        for half in range(2):
            slabs = [v[(2 * part + half) * per : (2 * part + half + 1) * per] for part in range(4)]
            out_ref[4 * per * group : 4 * per * (group + 1), half * LANES : (half + 1) * LANES] = jnp.concatenate(
                slabs, axis=0
            ).astype(jnp.bfloat16)
    positive = pos_ref[...]
    count = positive.shape[1]
    step = jnp.floor(positive.astype(jnp.float32) * (1.0 / count))
    row = positive.astype(jnp.float32) - step * count
    lines = lax.broadcasted_iota(jnp.int32, (TAIL, count), 0)
    out_ref[width:, :] = jnp.where(lines == 0, step, jnp.where(lines == 1, row, 0.0)).astype(jnp.bfloat16)


def repack(per, x_ref, packed_ref):
    for pair in range(packed_ref.shape[0] // (4 * per)):
        slabs = []
        for part in range(2):
            for half in range(2):
                v = x_ref[2 * per * pair : 2 * per * (pair + 1), half * LANES : (half + 1) * LANES]
                slabs.append(v[part * per : (part + 1) * per])
        packed_ref[4 * per * pair : 4 * per * (pair + 1), :] = jnp.concatenate(slabs, axis=0).astype(jnp.bfloat16)


def spread_kernel(per, packed_ref, out_ref):
    for pair in range(packed_ref.shape[0] // (4 * per)):
        v = packed_ref[4 * per * pair : 4 * per * (pair + 1), :].astype(jnp.float32)
        for part in range(4):
            at = (4 * pair + part) * LANES
            out_ref[:, at : at + LANES] = v[part * per : (part + 1) * per].astype(jnp.bfloat16)


def inv_rows(block):
    wide = block.astype(jnp.float32)
    return lax.rsqrt(jnp.sum(wide * wide, axis=1, keepdims=True) + EPS)


def inv_cols(block):
    wide = block.astype(jnp.float32)
    return lax.rsqrt(jnp.sum(wide * wide, axis=0, keepdims=True) + EPS)


def read_images(ref):
    width = ref.shape[0] - TAIL
    tail = ref[width:, :].astype(jnp.float32)
    positive = (tail[0:1] * ref.shape[1] + tail[1:2]).astype(jnp.int32)
    xb = ref[:width, :]
    return xb, inv_cols(xb), positive


def signs(positive, offset, shape):
    rows = lax.broadcasted_iota(jnp.int32, shape, 0)
    return positive == offset * shape[0] + rows


def scale_of(log_scale_ref):
    return jnp.exp(jnp.full((1, 1), log_scale_ref[0], jnp.float32))


def meet(scale, bias, raw, inv_txt, inv_img, hit):
    logits = raw * (scale * inv_txt) * inv_img + bias
    growth = jnp.exp(jnp.where(hit, -logits, logits))
    sig = growth / (1.0 + growth)
    return growth, jnp.where(hit, -sig, sig)


def softplus_sum(growth):
    parts = jnp.split(growth, 4, axis=0)
    while len(parts) > 1:
        parts = [a + b + a * b for a, b in zip(parts[::2], parts[1::2])]
    return jnp.sum(jnp.log1p(parts[0]), axis=0, keepdims=True)


def image_visit(scale, bias, block, xb, inv_img, positive, offset, inv_txt):
    raw = dot(block, xb, NN)
    growth, slope = meet(scale, bias, raw, inv_txt, inv_img, signs(positive, offset, raw.shape))
    weight = (slope * inv_txt).astype(jnp.bfloat16)
    along = jnp.sum(weight.astype(jnp.float32) * raw, axis=0, keepdims=True)
    return dot(weight, block, TN), softplus_sum(growth), along


def arrived_kernel(block_ref, out_ref):
    out_ref[...] = jnp.zeros(out_ref.shape, jnp.float32)


def norms_kernel(own_ref, back2_ref, out_ref):
    lanes = lax.broadcasted_iota(jnp.int32, out_ref.shape, 1)
    out_ref[...] = jnp.where(lanes == 0, inv_rows(own_ref[...]), inv_rows(back2_ref[...]))


def near_kernel(block_ref, out_ref):
    out_ref[...] = block_ref[...]


def early_kernel(log_scale_ref, bias_ref, image_ref, own_ref, back2_ref, norms_ref, acc_ref, loss_ref, along_ref):
    scale, bias = scale_of(log_scale_ref), bias_ref[0]
    xb, inv_img, positive = read_images(image_ref)
    part, loss, along = image_visit(scale, bias, own_ref[...], xb, inv_img, positive, 0, norms_ref[:, 0:1])
    acc_ref[...] = part
    part, loss2, along2 = image_visit(scale, bias, back2_ref[...], xb, inv_img, positive, 2, norms_ref[:, 1:2])
    acc_ref[...] += part
    loss_ref[...] = loss + loss2
    along_ref[...] = along + along2


def pick(odd, when_odd_ref, when_even_ref):
    return jnp.where(odd == 1, when_odd_ref[...], when_even_ref[...])


def late_kernel(
    per, parity_ref, log_scale_ref, bias_ref, image_ref, early_ref, early_loss_ref, early_along_ref, swap_ref,
    back1_ref, back3_ref, loss_ref, grad_ref, acc_ref, x_ref,
):
    scale, bias = scale_of(log_scale_ref), bias_ref[0]
    xb, inv_img, positive = read_images(image_ref)
    prev = pick(parity_ref[0], swap_ref, back1_ref)
    part, loss, along = image_visit(scale, bias, prev, xb, inv_img, positive, 1, inv_rows(prev))
    acc_ref[...] = early_ref[...] + part
    back3 = back3_ref[...]
    part, loss3, along3 = image_visit(scale, bias, back3, xb, inv_img, positive, 3, inv_rows(back3))
    acc_ref[...] += part
    loss_ref[...] = (early_loss_ref[...] + loss + loss3) * (1.0 / (STEPS * back3_ref.shape[0]))
    inner = (early_along_ref[...] + along + along3) * inv_img * inv_img
    x_ref[...] = (scale * inv_img) * (acc_ref[...].T - xb.astype(jnp.float32) * inner)
    repack(per, x_ref, grad_ref)


def text_visit(scale, bias, block, inv_txt, images, offset):
    xb, inv_img, positive = images
    raw = dot(block, xb, NN)
    slope = meet(scale, bias, raw, inv_txt, inv_img, signs(positive, offset, raw.shape))[1]
    return dot((slope * inv_img).astype(jnp.bfloat16), xb, NT)


def text_own_kernel(
    parity_ref, log_scale_ref, bias_ref, swap_ref, back1_ref, image_ref, after_ref, acc_ref, inv_ref, prev_ref
):
    scale, bias = scale_of(log_scale_ref), bias_ref[0]
    prev = pick(parity_ref[0], swap_ref, back1_ref)
    prev_ref[...] = prev
    inv_prev = inv_rows(prev)
    inv_ref[...] = inv_prev
    acc_ref[...] = text_visit(scale, bias, prev, inv_prev, read_images(image_ref), 1)


def text_send_kernel(log_scale_ref, bias_ref, prev_ref, inv_ref, acc_ref, img_next_ref, send_ref):
    scale, bias = scale_of(log_scale_ref), bias_ref[0]
    total = acc_ref[...] + text_visit(scale, bias, prev_ref[...], inv_ref[...], read_images(img_next_ref), 3)
    send_ref[...] = total.astype(jnp.bfloat16)


def text_local_kernel(log_scale_ref, bias_ref, own_ref, image_ref, img_next_ref, after_ref, local_ref):
    scale, bias = scale_of(log_scale_ref), bias_ref[0]
    own = own_ref[...]
    inv_own = inv_rows(own)
    local_ref[...] = text_visit(scale, bias, own, inv_own, read_images(image_ref), 0)
    local_ref[...] += text_visit(scale, bias, own, inv_own, read_images(img_next_ref), 2)


def finish_kernel(log_scale_ref, own_ref, got_ref, local_ref, out_ref, grad_ref, out_sem):
    scale = scale_of(log_scale_ref)
    parts = out_sem.shape[0]
    rows = out_ref.shape[0] // parts

    def store(i):
        at = pl.ds(rows * i, rows)
        return pltpu.make_async_copy(grad_ref.at[at], out_ref.at[at], out_sem.at[i])

    for i in range(parts):
        at = pl.ds(rows * i, rows)
        own = own_ref[at]
        inv = inv_rows(own)
        y = own.astype(jnp.float32) * inv
        grad = scale * (got_ref[at].astype(jnp.float32) + local_ref[at])
        grad_ref[at] = inv * (grad - y * jnp.sum(y * grad, axis=1, keepdims=True))
        store(i).start()
    for i in range(parts):
        store(i).wait()


HBM = pl.BlockSpec(memory_space=pltpu.HBM)
SMEM = pl.BlockSpec(memory_space=pltpu.SMEM)
VMEM = pl.BlockSpec(memory_space=pltpu.VMEM)


def call(kernel, out_shape, in_specs, scratch, flops, moved, out_spec=None, limit=VMEM_BYTES):
    several = isinstance(out_shape, (list, tuple))
    return pl.pallas_call(
        kernel,
        out_shape=out_shape,
        in_specs=in_specs,
        out_specs=tuple(VMEM for _ in out_shape) if several else out_spec or VMEM,
        scratch_shapes=scratch,
        compiler_params=pltpu.CompilerParams(vmem_limit_bytes=limit),
        cost_estimate=pl.CostEstimate(flops=flops, bytes_accessed=moved, transcendentals=0),
    )


def shards(images, texts, positive, log_scale, bias):
    per = images.shape[0]
    rows, width = texts.shape
    ranks = lax.axis_size("mp")
    packed_rows = width * rows // LANES
    parity = lax.rem(lax.axis_index("batch"), 2).reshape((1,))
    place = positive.reshape((1, rows))
    flat = jax.ShapeDtypeStruct((packed_rows, LANES), jnp.bfloat16)
    block_bytes = rows * width * 2
    task = 2 * rows * rows * width

    square = jax.ShapeDtypeStruct((rows, width), jnp.float32)
    line = jax.ShapeDtypeStruct((1, rows), jnp.float32)
    block = jax.ShapeDtypeStruct((rows, width), jnp.bfloat16)
    tall = jax.ShapeDtypeStruct((width + TAIL, rows), jnp.bfloat16)
    scalars = (parity, log_scale, bias)

    back2 = hop(texts, 2)
    swapped = swap(texts)
    packed = call(functools.partial(pack_kernel, per), flat, [HBM], [
            pltpu.VMEM(images.shape, jnp.bfloat16),
            pltpu.VMEM(flat.shape, jnp.bfloat16),
            pltpu.SemaphoreType.DMA((PARTS,)),
            pltpu.SemaphoreType.DMA((PARTS,)),
        ], 0, 2 * block_bytes, HBM, 60 * 1024 * 1024)(images)
    back3 = hop(back2, 1)
    back1 = hop(swapped, 2, 0)

    packed = lax.all_to_all(packed, "mp", split_axis=0, concat_axis=0, tiled=True)
    column = jax.ShapeDtypeStruct((rows, 1), jnp.float32)
    tile = jax.ShapeDtypeStruct((8, LANES), jnp.float32)
    pair = jax.ShapeDtypeStruct((rows, LANES), jnp.float32)
    arrived = call(arrived_kernel, tile, [HBM], [], 10_000_000_000, block_bytes)(back2)
    near2 = call(near_kernel, block, [VMEM], [], 1_000_000_000, 2 * block_bytes)(back2)
    norms = call(norms_kernel, pair, [VMEM] * 2, [], 1_000_000_000, 2 * block_bytes)(texts, near2)
    image = call(functools.partial(gather_kernel, per), tall, [VMEM] * 3, [], 0, 2 * block_bytes)(
        packed, place, arrived
    )
    image_next = hop(image, -2)

    early, early_loss, early_along = call(
        early_kernel, (square, line, line), [SMEM] * 2 + [VMEM] * 4, [], 4 * task, 5 * block_bytes
    )(log_scale, bias, image, texts, near2, norms)
    loss, grad = call(
        functools.partial(late_kernel, per),
        (line, flat),
        [SMEM] * 3 + [VMEM] * 7,
        [pltpu.VMEM((rows, width), jnp.float32), pltpu.VMEM((width, rows), jnp.float32)],
        4 * task,
        7 * block_bytes,
    )(*scalars, image, early, early_loss, early_along, swapped, back1, back3)
    image_grad = lax.all_to_all(grad, "mp", split_axis=0, concat_axis=0, tiled=True)

    text_own, inv_prev, prev = call(
        text_own_kernel, (square, column, block), [SMEM] * 3 + [VMEM] * 4, [], 2 * task, 4 * block_bytes
    )(*scalars, swapped, back1, image, loss)
    send = call(text_send_kernel, block, [SMEM] * 2 + [VMEM] * 4, [], 2 * task, 5 * block_bytes)(
        log_scale, bias, prev, inv_prev, text_own, image_next
    )
    got = hop(send, -1)
    local = call(text_local_kernel, square, [SMEM] * 2 + [VMEM] * 4, [], 4 * task, 5 * block_bytes)(
        log_scale, bias, texts, image, image_next, send
    )
    text_grad = call(
        finish_kernel,
        square,
        [SMEM, VMEM, VMEM, VMEM],
        [
            pltpu.VMEM((rows, width), jnp.float32),
            pltpu.SemaphoreType.DMA((PARTS,)),
        ],
        0,
        6 * block_bytes,
        HBM,
    )(log_scale, texts, got, local)

    wide = jax.ShapeDtypeStruct((per, ranks * rows), jnp.bfloat16)
    image_grad = call(functools.partial(spread_kernel, per), wide, [VMEM], [], 0, 2 * block_bytes)(image_grad)
    return (loss.reshape((rows,)), image_grad, text_grad)


def solution(mesh):
    in_specs = (P("mp", "batch"), P(("batch", "mp"), None), P(("batch", "mp")), P(), P())
    out_specs = (P(("batch", "mp")), P("mp", "batch"), P(("batch", "mp"), None))
    return jax.shard_map(shards, mesh=mesh, in_specs=in_specs, out_specs=out_specs, check_vma=False)
```

```python
import functools

import jax
import jax.numpy as jnp
from jax import lax
from jax.experimental import pallas as pl
from jax.experimental.pallas import tpu as pltpu
from jax.sharding import PartitionSpec as P

STEPS = 4
EPS = 1e-06
LANES = 128
TAIL = 16
PARTS = 4
VMEM_BYTES = 24 * 1024 * 1024

TN = (((0,), (0,)), ((), ()))
NT = (((1,), (1,)), ((), ()))
NN = (((1,), (0,)), ((), ()))


def hop(value, steps, parity=None):
    count = lax.axis_size("batch")
    pairs = [(s, (s + steps) % count) for s in range(count) if parity is None or s % 2 == parity]
    return lax.ppermute(value, "batch", pairs)


def swap(value):
    count = lax.axis_size("batch")
    return lax.ppermute(value, "batch", [(s, s ^ 1) for s in range(count)])


def dot(a, b, dims):
    return lax.dot_general(a, b, dims, preferred_element_type=jnp.float32)


def pack_kernel(per, images_ref, out_ref, in_ref, packed_ref, in_sem, out_sem):
    parts = in_sem.shape[0]
    columns = images_ref.shape[1] // parts
    lines = out_ref.shape[0] // parts

    def load(i):
        at = pl.ds(columns * i, columns)
        return pltpu.make_async_copy(images_ref.at[:, at], in_ref.at[:, at], in_sem.at[i])

    def store(i):
        at = pl.ds(lines * i, lines)
        return pltpu.make_async_copy(packed_ref.at[at], out_ref.at[at], out_sem.at[i])

    for i in range(parts):
        load(i).start()
    for i in range(parts):
        load(i).wait()
        for pair in range(columns * i // (4 * LANES), columns * (i + 1) // (4 * LANES)):
            slabs = []
            for part in range(4):
                at = (4 * pair + part) * LANES
                slabs.append(in_ref[:, at : at + LANES].astype(jnp.float32))
            packed_ref[4 * per * pair : 4 * per * (pair + 1), :] = jnp.concatenate(slabs, axis=0).astype(jnp.bfloat16)
        store(i).start()
    for i in range(parts):
        store(i).wait()


def gather_kernel(per, packed_ref, pos_ref, after_ref, out_ref):
    width = packed_ref.shape[0] // 2
    for group in range(width // (4 * per)):
        v = packed_ref[8 * per * group : 8 * per * (group + 1), :].astype(jnp.float32)
        for half in range(2):
            slabs = [v[(2 * part + half) * per : (2 * part + half + 1) * per] for part in range(4)]
            out_ref[4 * per * group : 4 * per * (group + 1), half * LANES : (half + 1) * LANES] = jnp.concatenate(
                slabs, axis=0
            ).astype(jnp.bfloat16)
    positive = pos_ref[...]
    count = positive.shape[1]
    step = jnp.floor(positive.astype(jnp.float32) * (1.0 / count))
    row = positive.astype(jnp.float32) - step * count
    lines = lax.broadcasted_iota(jnp.int32, (TAIL, count), 0)
    out_ref[width:, :] = jnp.where(lines == 0, step, jnp.where(lines == 1, row, 0.0)).astype(jnp.bfloat16)


def repack(per, x_ref, packed_ref):
    for pair in range(packed_ref.shape[0] // (4 * per)):
        slabs = []
        for part in range(2):
            for half in range(2):
                v = x_ref[2 * per * pair : 2 * per * (pair + 1), half * LANES : (half + 1) * LANES]
                slabs.append(v[part * per : (part + 1) * per])
        packed_ref[4 * per * pair : 4 * per * (pair + 1), :] = jnp.concatenate(slabs, axis=0).astype(jnp.bfloat16)


def spread_kernel(per, packed_ref, out_ref):
    for pair in range(packed_ref.shape[0] // (4 * per)):
        v = packed_ref[4 * per * pair : 4 * per * (pair + 1), :].astype(jnp.float32)
        for part in range(4):
            at = (4 * pair + part) * LANES
            out_ref[:, at : at + LANES] = v[part * per : (part + 1) * per].astype(jnp.bfloat16)


def inv_rows(block):
    wide = block.astype(jnp.float32)
    return lax.rsqrt(jnp.sum(wide * wide, axis=1, keepdims=True) + EPS)


def inv_cols(block):
    wide = block.astype(jnp.float32)
    return lax.rsqrt(jnp.sum(wide * wide, axis=0, keepdims=True) + EPS)


def read_images(ref):
    width = ref.shape[0] - TAIL
    tail = ref[width:, :].astype(jnp.float32)
    positive = (tail[0:1] * ref.shape[1] + tail[1:2]).astype(jnp.int32)
    xb = ref[:width, :]
    return xb, inv_cols(xb), positive


def signs(positive, offset, shape):
    rows = lax.broadcasted_iota(jnp.int32, shape, 0)
    return positive == offset * shape[0] + rows


def scale_of(log_scale_ref):
    return jnp.exp(jnp.full((1, 1), log_scale_ref[0], jnp.float32))


def meet(scale, bias, raw, inv_txt, inv_img, hit):
    logits = raw * (scale * inv_txt) * inv_img + bias
    growth = jnp.exp(jnp.where(hit, -logits, logits))
    sig = growth / (1.0 + growth)
    return growth, jnp.where(hit, -sig, sig)


def softplus_sum(growth):
    parts = jnp.split(growth, 4, axis=0)
    while len(parts) > 1:
        parts = [a + b + a * b for a, b in zip(parts[::2], parts[1::2])]
    return jnp.sum(jnp.log1p(parts[0]), axis=0, keepdims=True)


def image_visit(scale, bias, block, xb, inv_img, positive, offset, inv_txt):
    raw = dot(block, xb, NN)
    growth, slope = meet(scale, bias, raw, inv_txt, inv_img, signs(positive, offset, raw.shape))
    weight = (slope * inv_txt).astype(jnp.bfloat16)
    along = jnp.sum(weight.astype(jnp.float32) * raw, axis=0, keepdims=True)
    return dot(weight, block, TN), softplus_sum(growth), along


def arrived_kernel(block_ref, out_ref):
    out_ref[...] = jnp.zeros(out_ref.shape, jnp.float32)


def norms_kernel(own_ref, back2_ref, out_ref):
    lanes = lax.broadcasted_iota(jnp.int32, out_ref.shape, 1)
    out_ref[...] = jnp.where(lanes == 0, inv_rows(own_ref[...]), inv_rows(back2_ref[...]))


def near_kernel(block_ref, out_ref):
    out_ref[...] = block_ref[...]


def pick_kernel(parity_ref, swap_ref, back1_ref, after_ref, prev_ref):
    prev_ref[...] = pick(parity_ref[0], swap_ref, back1_ref)


def early_kernel(log_scale_ref, bias_ref, image_ref, own_ref, back2_ref, norms_ref, acc_ref, loss_ref, along_ref):
    scale, bias = scale_of(log_scale_ref), bias_ref[0]
    xb, inv_img, positive = read_images(image_ref)
    part, loss, along = image_visit(scale, bias, own_ref[...], xb, inv_img, positive, 0, norms_ref[:, 0:1])
    acc_ref[...] = part
    part, loss2, along2 = image_visit(scale, bias, back2_ref[...], xb, inv_img, positive, 2, norms_ref[:, 1:2])
    acc_ref[...] += part
    loss_ref[...] = loss + loss2
    along_ref[...] = along + along2


def pick(odd, when_odd_ref, when_even_ref):
    return jnp.where(odd == 1, when_odd_ref[...], when_even_ref[...])


def late_kernel(
    per, log_scale_ref, bias_ref, image_ref, early_ref, early_loss_ref, early_along_ref, prev_ref,
    back3_ref, loss_ref, grad_ref, acc_ref, x_ref,
):
    scale, bias = scale_of(log_scale_ref), bias_ref[0]
    xb, inv_img, positive = read_images(image_ref)
    prev = prev_ref[...]
    part, loss, along = image_visit(scale, bias, prev, xb, inv_img, positive, 1, inv_rows(prev))
    acc_ref[...] = early_ref[...] + part
    back3 = back3_ref[...]
    part, loss3, along3 = image_visit(scale, bias, back3, xb, inv_img, positive, 3, inv_rows(back3))
    acc_ref[...] += part
    loss_ref[...] = (early_loss_ref[...] + loss + loss3) * (1.0 / (STEPS * back3_ref.shape[0]))
    inner = (early_along_ref[...] + along + along3) * inv_img * inv_img
    x_ref[...] = (scale * inv_img) * (acc_ref[...].T - xb.astype(jnp.float32) * inner)
    repack(per, x_ref, grad_ref)


def text_visit(scale, bias, block, inv_txt, images, offset):
    xb, inv_img, positive = images
    raw = dot(block, xb, NN)
    slope = meet(scale, bias, raw, inv_txt, inv_img, signs(positive, offset, raw.shape))[1]
    return dot((slope * inv_img).astype(jnp.bfloat16), xb, NT)


def text_own_kernel(
    log_scale_ref, bias_ref, prev_ref, image_ref, after_ref, acc_ref, inv_ref
):
    scale, bias = scale_of(log_scale_ref), bias_ref[0]
    prev = prev_ref[...]
    inv_prev = inv_rows(prev)
    inv_ref[...] = inv_prev
    acc_ref[...] = text_visit(scale, bias, prev, inv_prev, read_images(image_ref), 1)


def text_send_kernel(log_scale_ref, bias_ref, prev_ref, inv_ref, acc_ref, img_next_ref, send_ref):
    scale, bias = scale_of(log_scale_ref), bias_ref[0]
    total = acc_ref[...] + text_visit(scale, bias, prev_ref[...], inv_ref[...], read_images(img_next_ref), 3)
    send_ref[...] = total.astype(jnp.bfloat16)


def text_local_kernel(log_scale_ref, bias_ref, own_ref, image_ref, img_next_ref, after_ref, local_ref):
    scale, bias = scale_of(log_scale_ref), bias_ref[0]
    own = own_ref[...]
    inv_own = inv_rows(own)
    local_ref[...] = text_visit(scale, bias, own, inv_own, read_images(image_ref), 0)
    local_ref[...] += text_visit(scale, bias, own, inv_own, read_images(img_next_ref), 2)


def finish_kernel(log_scale_ref, own_ref, got_ref, local_ref, out_ref, grad_ref, out_sem):
    scale = scale_of(log_scale_ref)
    parts = out_sem.shape[0]
    rows = out_ref.shape[0] // parts

    def store(i):
        at = pl.ds(rows * i, rows)
        return pltpu.make_async_copy(grad_ref.at[at], out_ref.at[at], out_sem.at[i])

    for i in range(parts):
        at = pl.ds(rows * i, rows)
        own = own_ref[at]
        inv = inv_rows(own)
        y = own.astype(jnp.float32) * inv
        grad = scale * (got_ref[at].astype(jnp.float32) + local_ref[at])
        grad_ref[at] = inv * (grad - y * jnp.sum(y * grad, axis=1, keepdims=True))
        store(i).start()
    for i in range(parts):
        store(i).wait()


HBM = pl.BlockSpec(memory_space=pltpu.HBM)
SMEM = pl.BlockSpec(memory_space=pltpu.SMEM)
VMEM = pl.BlockSpec(memory_space=pltpu.VMEM)


def call(kernel, out_shape, in_specs, scratch, flops, moved, out_spec=None, limit=VMEM_BYTES):
    several = isinstance(out_shape, (list, tuple))
    return pl.pallas_call(
        kernel,
        out_shape=out_shape,
        in_specs=in_specs,
        out_specs=tuple(VMEM for _ in out_shape) if several else out_spec or VMEM,
        scratch_shapes=scratch,
        compiler_params=pltpu.CompilerParams(vmem_limit_bytes=limit),
        cost_estimate=pl.CostEstimate(flops=flops, bytes_accessed=moved, transcendentals=0),
    )


def shards(images, texts, positive, log_scale, bias):
    per = images.shape[0]
    rows, width = texts.shape
    ranks = lax.axis_size("mp")
    packed_rows = width * rows // LANES
    parity = lax.rem(lax.axis_index("batch"), 2).reshape((1,))
    place = positive.reshape((1, rows))
    flat = jax.ShapeDtypeStruct((packed_rows, LANES), jnp.bfloat16)
    block_bytes = rows * width * 2
    task = 2 * rows * rows * width

    square = jax.ShapeDtypeStruct((rows, width), jnp.float32)
    line = jax.ShapeDtypeStruct((1, rows), jnp.float32)
    block = jax.ShapeDtypeStruct((rows, width), jnp.bfloat16)
    tall = jax.ShapeDtypeStruct((width + TAIL, rows), jnp.bfloat16)

    back2 = hop(texts, 2)
    swapped = swap(texts)
    packed = call(functools.partial(pack_kernel, per), flat, [HBM], [
            pltpu.VMEM(images.shape, jnp.bfloat16),
            pltpu.VMEM(flat.shape, jnp.bfloat16),
            pltpu.SemaphoreType.DMA((PARTS,)),
            pltpu.SemaphoreType.DMA((PARTS,)),
        ], 0, 2 * block_bytes, HBM, 60 * 1024 * 1024)(images)
    back3 = hop(back2, 1)
    back1 = hop(swapped, 2, 0)

    packed = lax.all_to_all(packed, "mp", split_axis=0, concat_axis=0, tiled=True)
    column = jax.ShapeDtypeStruct((rows, 1), jnp.float32)
    tile = jax.ShapeDtypeStruct((8, LANES), jnp.float32)
    pair = jax.ShapeDtypeStruct((rows, LANES), jnp.float32)
    arrived = call(arrived_kernel, tile, [HBM], [], 10_000_000_000, block_bytes)(back2)
    near2 = call(near_kernel, block, [VMEM], [], 1_000_000_000, 2 * block_bytes)(back2)
    norms = call(norms_kernel, pair, [VMEM] * 2, [], 1_000_000_000, 2 * block_bytes)(texts, near2)
    image = call(functools.partial(gather_kernel, per), tall, [VMEM] * 3, [], 0, 2 * block_bytes)(
        packed, place, arrived
    )
    image_next = hop(image, -2)

    arrived3 = call(arrived_kernel, tile, [HBM], [], 1_000_000_000, block_bytes)(back3)
    prev = call(pick_kernel, block, [SMEM] + [VMEM] * 3, [], 0, 3 * block_bytes)(parity, swapped, back1, arrived3)
    early, early_loss, early_along = call(
        early_kernel, (square, line, line), [SMEM] * 2 + [VMEM] * 4, [], 4 * task, 5 * block_bytes
    )(log_scale, bias, image, texts, near2, norms)
    loss, grad = call(
        functools.partial(late_kernel, per),
        (line, flat),
        [SMEM] * 2 + [VMEM] * 6,
        [pltpu.VMEM((rows, width), jnp.float32), pltpu.VMEM((width, rows), jnp.float32)],
        4 * task,
        7 * block_bytes,
    )(log_scale, bias, image, early, early_loss, early_along, prev, back3)
    image_grad = lax.all_to_all(grad, "mp", split_axis=0, concat_axis=0, tiled=True)

    text_own, inv_prev = call(
        text_own_kernel, (square, column), [SMEM] * 2 + [VMEM] * 3, [], 2 * task, 4 * block_bytes
    )(log_scale, bias, prev, image, loss)
    send = call(text_send_kernel, block, [SMEM] * 2 + [VMEM] * 4, [], 2 * task, 5 * block_bytes)(
        log_scale, bias, prev, inv_prev, text_own, image_next
    )
    got = hop(send, -1)
    local = call(text_local_kernel, square, [SMEM] * 2 + [VMEM] * 4, [], 4 * task, 5 * block_bytes)(
        log_scale, bias, texts, image, image_next, send
    )
    text_grad = call(
        finish_kernel,
        square,
        [SMEM, VMEM, VMEM, VMEM],
        [
            pltpu.VMEM((rows, width), jnp.float32),
            pltpu.SemaphoreType.DMA((PARTS,)),
        ],
        0,
        6 * block_bytes,
        HBM,
    )(log_scale, texts, got, local)

    wide = jax.ShapeDtypeStruct((per, ranks * rows), jnp.bfloat16)
    image_grad = call(functools.partial(spread_kernel, per), wide, [VMEM], [], 0, 2 * block_bytes)(image_grad)
    return (loss.reshape((rows,)), image_grad, text_grad)


def solution(mesh):
    in_specs = (P("mp", "batch"), P(("batch", "mp"), None), P(("batch", "mp")), P(), P())
    out_specs = (P(("batch", "mp")), P("mp", "batch"), P(("batch", "mp"), None))
    return jax.shard_map(shards, mesh=mesh, in_specs=in_specs, out_specs=out_specs, check_vma=False)
```

```python
import functools

import jax
import jax.numpy as jnp
from jax import lax
from jax.experimental import pallas as pl
from jax.experimental.pallas import tpu as pltpu
from jax.sharding import PartitionSpec as P

STEPS = 4
EPS = 1e-06
LANES = 128
TAIL = 16
PARTS = 4
VMEM_BYTES = 24 * 1024 * 1024

TN = (((0,), (0,)), ((), ()))
NT = (((1,), (1,)), ((), ()))
NN = (((1,), (0,)), ((), ()))


def hop(value, steps, parity=None):
    count = lax.axis_size("batch")
    pairs = [(s, (s + steps) % count) for s in range(count) if parity is None or s % 2 == parity]
    return lax.ppermute(value, "batch", pairs)


def swap(value):
    count = lax.axis_size("batch")
    return lax.ppermute(value, "batch", [(s, s ^ 1) for s in range(count)])


def dot(a, b, dims):
    return lax.dot_general(a, b, dims, preferred_element_type=jnp.float32)


def pack_kernel(per, images_ref, out_ref, in_ref, packed_ref, in_sem, out_sem):
    parts = in_sem.shape[0]
    columns = images_ref.shape[1] // parts
    lines = out_ref.shape[0] // parts

    def load(i):
        at = pl.ds(columns * i, columns)
        return pltpu.make_async_copy(images_ref.at[:, at], in_ref.at[:, at], in_sem.at[i])

    def store(i):
        at = pl.ds(lines * i, lines)
        return pltpu.make_async_copy(packed_ref.at[at], out_ref.at[at], out_sem.at[i])

    for i in range(parts):
        load(i).start()
    for i in range(parts):
        load(i).wait()
        for pair in range(columns * i // (4 * LANES), columns * (i + 1) // (4 * LANES)):
            slabs = []
            for part in range(4):
                at = (4 * pair + part) * LANES
                slabs.append(in_ref[:, at : at + LANES].astype(jnp.float32))
            packed_ref[4 * per * pair : 4 * per * (pair + 1), :] = jnp.concatenate(slabs, axis=0).astype(jnp.bfloat16)
        store(i).start()
    for i in range(parts):
        store(i).wait()


def gather_kernel(per, packed_ref, pos_ref, after_ref, out_ref):
    width = packed_ref.shape[0] // 2
    for group in range(width // (4 * per)):
        v = packed_ref[8 * per * group : 8 * per * (group + 1), :].astype(jnp.float32)
        for half in range(2):
            slabs = [v[(2 * part + half) * per : (2 * part + half + 1) * per] for part in range(4)]
            out_ref[4 * per * group : 4 * per * (group + 1), half * LANES : (half + 1) * LANES] = jnp.concatenate(
                slabs, axis=0
            ).astype(jnp.bfloat16)
    positive = pos_ref[...]
    count = positive.shape[1]
    step = jnp.floor(positive.astype(jnp.float32) * (1.0 / count))
    row = positive.astype(jnp.float32) - step * count
    lines = lax.broadcasted_iota(jnp.int32, (TAIL, count), 0)
    out_ref[width:, :] = jnp.where(lines == 0, step, jnp.where(lines == 1, row, 0.0)).astype(jnp.bfloat16)


def repack(per, x_ref, packed_ref):
    for pair in range(packed_ref.shape[0] // (4 * per)):
        slabs = []
        for part in range(2):
            for half in range(2):
                v = x_ref[2 * per * pair : 2 * per * (pair + 1), half * LANES : (half + 1) * LANES]
                slabs.append(v[part * per : (part + 1) * per])
        packed_ref[4 * per * pair : 4 * per * (pair + 1), :] = jnp.concatenate(slabs, axis=0).astype(jnp.bfloat16)


def spread_kernel(per, packed_ref, out_ref):
    for pair in range(packed_ref.shape[0] // (4 * per)):
        v = packed_ref[4 * per * pair : 4 * per * (pair + 1), :].astype(jnp.float32)
        for part in range(4):
            at = (4 * pair + part) * LANES
            out_ref[:, at : at + LANES] = v[part * per : (part + 1) * per].astype(jnp.bfloat16)


def inv_rows(block):
    wide = block.astype(jnp.float32)
    return lax.rsqrt(jnp.sum(wide * wide, axis=1, keepdims=True) + EPS)


def inv_cols(block):
    wide = block.astype(jnp.float32)
    return lax.rsqrt(jnp.sum(wide * wide, axis=0, keepdims=True) + EPS)


def read_images(ref):
    width = ref.shape[0] - TAIL
    tail = ref[width:, :].astype(jnp.float32)
    positive = (tail[0:1] * ref.shape[1] + tail[1:2]).astype(jnp.int32)
    xb = ref[:width, :]
    return xb, inv_cols(xb), positive


def signs(positive, offset, shape):
    rows = lax.broadcasted_iota(jnp.int32, shape, 0)
    return positive == offset * shape[0] + rows


def scale_of(log_scale_ref):
    return jnp.exp(jnp.full((1, 1), log_scale_ref[0], jnp.float32))


def meet(scale, bias, raw, inv_txt, inv_img, hit):
    logits = raw * (scale * inv_txt) * inv_img + bias
    growth = jnp.exp(jnp.where(hit, -logits, logits))
    sig = growth / (1.0 + growth)
    return growth, jnp.where(hit, -sig, sig)


def softplus_sum(growth):
    parts = jnp.split(growth, 4, axis=0)
    while len(parts) > 1:
        parts = [a + b + a * b for a, b in zip(parts[::2], parts[1::2])]
    return jnp.sum(jnp.log1p(parts[0]), axis=0, keepdims=True)


def image_visit(scale, bias, block, xb, inv_img, positive, offset, inv_txt):
    raw = dot(block, xb, NN)
    growth, slope = meet(scale, bias, raw, inv_txt, inv_img, signs(positive, offset, raw.shape))
    weight = (slope * inv_txt).astype(jnp.bfloat16)
    along = jnp.sum(weight.astype(jnp.float32) * raw, axis=0, keepdims=True)
    return dot(weight, block, TN), softplus_sum(growth), along


def arrived_kernel(block_ref, out_ref):
    out_ref[...] = jnp.zeros(out_ref.shape, jnp.float32)


def norms_kernel(own_ref, back2_ref, out_ref):
    lanes = lax.broadcasted_iota(jnp.int32, out_ref.shape, 1)
    out_ref[...] = jnp.where(lanes == 0, inv_rows(own_ref[...]), inv_rows(back2_ref[...]))


def near_kernel(block_ref, out_ref):
    out_ref[...] = block_ref[...]


def pick_kernel(parity_ref, swap_ref, back1_ref, after_ref, prev_ref):
    prev_ref[...] = pick(parity_ref[0], swap_ref, back1_ref)


def early_kernel(log_scale_ref, bias_ref, image_ref, own_ref, back2_ref, norms_ref, acc_ref, loss_ref, along_ref):
    scale, bias = scale_of(log_scale_ref), bias_ref[0]
    xb, inv_img, positive = read_images(image_ref)
    part, loss, along = image_visit(scale, bias, own_ref[...], xb, inv_img, positive, 0, norms_ref[:, 0:1])
    acc_ref[...] = part
    part, loss2, along2 = image_visit(scale, bias, back2_ref[...], xb, inv_img, positive, 2, norms_ref[:, 1:2])
    acc_ref[...] += part
    loss_ref[...] = loss + loss2
    along_ref[...] = along + along2


def pick(odd, when_odd_ref, when_even_ref):
    return jnp.where(odd == 1, when_odd_ref[...], when_even_ref[...])


def late_kernel(
    per, log_scale_ref, bias_ref, image_ref, early_ref, early_loss_ref, early_along_ref, prev_ref,
    back3_ref, after_ref, loss_ref, grad_ref, acc_ref, x_ref,
):
    scale, bias = scale_of(log_scale_ref), bias_ref[0]
    xb, inv_img, positive = read_images(image_ref)
    prev = prev_ref[...]
    part, loss, along = image_visit(scale, bias, prev, xb, inv_img, positive, 1, inv_rows(prev))
    acc_ref[...] = early_ref[...] + part
    back3 = back3_ref[...]
    part, loss3, along3 = image_visit(scale, bias, back3, xb, inv_img, positive, 3, inv_rows(back3))
    acc_ref[...] += part
    loss_ref[...] = (early_loss_ref[...] + loss + loss3) * (1.0 / (STEPS * back3_ref.shape[0]))
    inner = (early_along_ref[...] + along + along3) * inv_img * inv_img
    x_ref[...] = (scale * inv_img) * (acc_ref[...].T - xb.astype(jnp.float32) * inner)
    repack(per, x_ref, grad_ref)


def text_visit(scale, bias, block, inv_txt, images, offset):
    xb, inv_img, positive = images
    raw = dot(block, xb, NN)
    slope = meet(scale, bias, raw, inv_txt, inv_img, signs(positive, offset, raw.shape))[1]
    return dot((slope * inv_img).astype(jnp.bfloat16), xb, NT)


def text_own_kernel(
    log_scale_ref, bias_ref, prev_ref, image_ref, after_ref, acc_ref, inv_ref
):
    scale, bias = scale_of(log_scale_ref), bias_ref[0]
    prev = prev_ref[...]
    inv_prev = inv_rows(prev)
    inv_ref[...] = inv_prev
    acc_ref[...] = text_visit(scale, bias, prev, inv_prev, read_images(image_ref), 1)


def text_send_kernel(log_scale_ref, bias_ref, prev_ref, inv_ref, acc_ref, img_next_ref, send_ref):
    scale, bias = scale_of(log_scale_ref), bias_ref[0]
    total = acc_ref[...] + text_visit(scale, bias, prev_ref[...], inv_ref[...], read_images(img_next_ref), 3)
    send_ref[...] = total.astype(jnp.bfloat16)


def text_local_kernel(log_scale_ref, bias_ref, own_ref, image_ref, img_next_ref, after_ref, local_ref):
    scale, bias = scale_of(log_scale_ref), bias_ref[0]
    own = own_ref[...]
    inv_own = inv_rows(own)
    local_ref[...] = text_visit(scale, bias, own, inv_own, read_images(image_ref), 0)
    local_ref[...] += text_visit(scale, bias, own, inv_own, read_images(img_next_ref), 2)


def finish_kernel(log_scale_ref, own_ref, got_ref, local_ref, out_ref, grad_ref, out_sem):
    scale = scale_of(log_scale_ref)
    parts = out_sem.shape[0]
    rows = out_ref.shape[0] // parts

    def store(i):
        at = pl.ds(rows * i, rows)
        return pltpu.make_async_copy(grad_ref.at[at], out_ref.at[at], out_sem.at[i])

    for i in range(parts):
        at = pl.ds(rows * i, rows)
        own = own_ref[at]
        inv = inv_rows(own)
        y = own.astype(jnp.float32) * inv
        grad = scale * (got_ref[at].astype(jnp.float32) + local_ref[at])
        grad_ref[at] = inv * (grad - y * jnp.sum(y * grad, axis=1, keepdims=True))
        store(i).start()
    for i in range(parts):
        store(i).wait()


HBM = pl.BlockSpec(memory_space=pltpu.HBM)
SMEM = pl.BlockSpec(memory_space=pltpu.SMEM)
VMEM = pl.BlockSpec(memory_space=pltpu.VMEM)


def call(kernel, out_shape, in_specs, scratch, flops, moved, out_spec=None, limit=VMEM_BYTES):
    several = isinstance(out_shape, (list, tuple))
    return pl.pallas_call(
        kernel,
        out_shape=out_shape,
        in_specs=in_specs,
        out_specs=tuple(VMEM for _ in out_shape) if several else out_spec or VMEM,
        scratch_shapes=scratch,
        compiler_params=pltpu.CompilerParams(vmem_limit_bytes=limit),
        cost_estimate=pl.CostEstimate(flops=flops, bytes_accessed=moved, transcendentals=0),
    )


def shards(images, texts, positive, log_scale, bias):
    per = images.shape[0]
    rows, width = texts.shape
    ranks = lax.axis_size("mp")
    packed_rows = width * rows // LANES
    parity = lax.rem(lax.axis_index("batch"), 2).reshape((1,))
    place = positive.reshape((1, rows))
    flat = jax.ShapeDtypeStruct((packed_rows, LANES), jnp.bfloat16)
    block_bytes = rows * width * 2
    task = 2 * rows * rows * width

    square = jax.ShapeDtypeStruct((rows, width), jnp.float32)
    line = jax.ShapeDtypeStruct((1, rows), jnp.float32)
    block = jax.ShapeDtypeStruct((rows, width), jnp.bfloat16)
    tall = jax.ShapeDtypeStruct((width + TAIL, rows), jnp.bfloat16)

    back2 = hop(texts, 2)
    swapped = swap(texts)
    packed = call(functools.partial(pack_kernel, per), flat, [HBM], [
            pltpu.VMEM(images.shape, jnp.bfloat16),
            pltpu.VMEM(flat.shape, jnp.bfloat16),
            pltpu.SemaphoreType.DMA((PARTS,)),
            pltpu.SemaphoreType.DMA((PARTS,)),
        ], 0, 2 * block_bytes, HBM, 60 * 1024 * 1024)(images)
    back3 = hop(back2, 1)
    back1 = hop(swapped, 2, 0)

    packed = lax.all_to_all(packed, "mp", split_axis=0, concat_axis=0, tiled=True)
    column = jax.ShapeDtypeStruct((rows, 1), jnp.float32)
    tile = jax.ShapeDtypeStruct((8, LANES), jnp.float32)
    pair = jax.ShapeDtypeStruct((rows, LANES), jnp.float32)
    arrived = call(arrived_kernel, tile, [HBM], [], 10_000_000_000, block_bytes)(back2)
    near2 = call(near_kernel, block, [VMEM], [], 1_000_000_000, 2 * block_bytes)(back2)
    norms = call(norms_kernel, pair, [VMEM] * 2, [], 1_000_000_000, 2 * block_bytes)(texts, near2)
    image = call(functools.partial(gather_kernel, per), tall, [VMEM] * 3, [], 0, 2 * block_bytes)(
        packed, place, arrived
    )
    image_next = hop(image, -2)

    arrived3 = call(arrived_kernel, tile, [HBM], [], 1_000_000_000, block_bytes)(back3)
    prev = call(pick_kernel, block, [SMEM] + [VMEM] * 3, [], 0, 3 * block_bytes)(parity, swapped, back1, arrived3)
    early, early_loss, early_along = call(
        early_kernel, (square, line, line), [SMEM] * 2 + [VMEM] * 4, [], 4 * task, 5 * block_bytes
    )(log_scale, bias, image, texts, near2, norms)
    loss, grad = call(
        functools.partial(late_kernel, per),
        (line, flat),
        [SMEM] * 2 + [VMEM] * 6 + [HBM],
        [pltpu.VMEM((rows, width), jnp.float32), pltpu.VMEM((width, rows), jnp.float32)],
        4 * task,
        7 * block_bytes,
    )(log_scale, bias, image, early, early_loss, early_along, prev, back3, back1)
    image_grad = lax.all_to_all(grad, "mp", split_axis=0, concat_axis=0, tiled=True)

    text_own, inv_prev = call(
        text_own_kernel, (square, column), [SMEM] * 2 + [VMEM] * 3, [], 2 * task, 4 * block_bytes
    )(log_scale, bias, prev, image, loss)
    send = call(text_send_kernel, block, [SMEM] * 2 + [VMEM] * 4, [], 2 * task, 5 * block_bytes)(
        log_scale, bias, prev, inv_prev, text_own, image_next
    )
    got = hop(send, -1)
    local = call(text_local_kernel, square, [SMEM] * 2 + [VMEM] * 4, [], 4 * task, 5 * block_bytes)(
        log_scale, bias, texts, image, image_next, send
    )
    text_grad = call(
        finish_kernel,
        square,
        [SMEM, VMEM, VMEM, VMEM],
        [
            pltpu.VMEM((rows, width), jnp.float32),
            pltpu.SemaphoreType.DMA((PARTS,)),
        ],
        0,
        6 * block_bytes,
        HBM,
    )(log_scale, texts, got, local)

    wide = jax.ShapeDtypeStruct((per, ranks * rows), jnp.bfloat16)
    image_grad = call(functools.partial(spread_kernel, per), wide, [VMEM], [], 0, 2 * block_bytes)(image_grad)
    return (loss.reshape((rows,)), image_grad, text_grad)


def solution(mesh):
    in_specs = (P("mp", "batch"), P(("batch", "mp"), None), P(("batch", "mp")), P(), P())
    out_specs = (P(("batch", "mp")), P("mp", "batch"), P(("batch", "mp"), None))
    return jax.shard_map(shards, mesh=mesh, in_specs=in_specs, out_specs=out_specs, check_vma=False)
```

```python
import functools

import jax
import jax.numpy as jnp
from jax import lax
from jax.experimental import pallas as pl
from jax.experimental.pallas import tpu as pltpu
from jax.sharding import PartitionSpec as P

STEPS = 4
EPS = 1e-06
LANES = 128
TAIL = 16
PARTS = 4
VMEM_BYTES = 24 * 1024 * 1024

TN = (((0,), (0,)), ((), ()))
NT = (((1,), (1,)), ((), ()))
NN = (((1,), (0,)), ((), ()))


def hop(value, steps, parity=None):
    count = lax.axis_size("batch")
    pairs = [(s, (s + steps) % count) for s in range(count) if parity is None or s % 2 == parity]
    return lax.ppermute(value, "batch", pairs)


def swap(value):
    count = lax.axis_size("batch")
    return lax.ppermute(value, "batch", [(s, s ^ 1) for s in range(count)])


def dot(a, b, dims):
    return lax.dot_general(a, b, dims, preferred_element_type=jnp.float32)


def pack_kernel(per, images_ref, out_ref, in_ref, packed_ref, in_sem, out_sem):
    parts = in_sem.shape[0]
    columns = images_ref.shape[1] // parts
    lines = out_ref.shape[0] // parts

    def load(i):
        at = pl.ds(columns * i, columns)
        return pltpu.make_async_copy(images_ref.at[:, at], in_ref.at[:, at], in_sem.at[i])

    def store(i):
        at = pl.ds(lines * i, lines)
        return pltpu.make_async_copy(packed_ref.at[at], out_ref.at[at], out_sem.at[i])

    for i in range(parts):
        load(i).start()
    for i in range(parts):
        load(i).wait()
        for pair in range(columns * i // (4 * LANES), columns * (i + 1) // (4 * LANES)):
            slabs = []
            for part in range(4):
                at = (4 * pair + part) * LANES
                slabs.append(in_ref[:, at : at + LANES].astype(jnp.float32))
            packed_ref[4 * per * pair : 4 * per * (pair + 1), :] = jnp.concatenate(slabs, axis=0).astype(jnp.bfloat16)
        store(i).start()
    for i in range(parts):
        store(i).wait()


def gather_kernel(per, packed_ref, pos_ref, after_ref, out_ref):
    width = packed_ref.shape[0] // 2
    for group in range(width // (4 * per)):
        v = packed_ref[8 * per * group : 8 * per * (group + 1), :].astype(jnp.float32)
        for half in range(2):
            slabs = [v[(2 * part + half) * per : (2 * part + half + 1) * per] for part in range(4)]
            out_ref[4 * per * group : 4 * per * (group + 1), half * LANES : (half + 1) * LANES] = jnp.concatenate(
                slabs, axis=0
            ).astype(jnp.bfloat16)
    positive = pos_ref[...]
    count = positive.shape[1]
    step = jnp.floor(positive.astype(jnp.float32) * (1.0 / count))
    row = positive.astype(jnp.float32) - step * count
    lines = lax.broadcasted_iota(jnp.int32, (TAIL, count), 0)
    out_ref[width:, :] = jnp.where(lines == 0, step, jnp.where(lines == 1, row, 0.0)).astype(jnp.bfloat16)


def repack(per, x_ref, packed_ref):
    for pair in range(packed_ref.shape[0] // (4 * per)):
        slabs = []
        for part in range(2):
            for half in range(2):
                v = x_ref[2 * per * pair : 2 * per * (pair + 1), half * LANES : (half + 1) * LANES]
                slabs.append(v[part * per : (part + 1) * per])
        packed_ref[4 * per * pair : 4 * per * (pair + 1), :] = jnp.concatenate(slabs, axis=0).astype(jnp.bfloat16)


def spread_kernel(per, packed_ref, out_ref):
    for pair in range(packed_ref.shape[0] // (4 * per)):
        v = packed_ref[4 * per * pair : 4 * per * (pair + 1), :].astype(jnp.float32)
        for part in range(4):
            at = (4 * pair + part) * LANES
            out_ref[:, at : at + LANES] = v[part * per : (part + 1) * per].astype(jnp.bfloat16)


def inv_rows(block):
    wide = block.astype(jnp.float32)
    return lax.rsqrt(jnp.sum(wide * wide, axis=1, keepdims=True) + EPS)


def inv_cols(block):
    wide = block.astype(jnp.float32)
    return lax.rsqrt(jnp.sum(wide * wide, axis=0, keepdims=True) + EPS)


def read_images(ref):
    width = ref.shape[0] - TAIL
    tail = ref[width:, :].astype(jnp.float32)
    positive = (tail[0:1] * ref.shape[1] + tail[1:2]).astype(jnp.int32)
    xb = ref[:width, :]
    return xb, inv_cols(xb), positive


def signs(positive, offset, shape):
    rows = lax.broadcasted_iota(jnp.int32, shape, 0)
    return positive == offset * shape[0] + rows


def scale_of(log_scale_ref):
    return jnp.exp(jnp.full((1, 1), log_scale_ref[0], jnp.float32))


def meet(scale, bias, raw, inv_txt, inv_img, hit):
    logits = raw * (scale * inv_txt) * inv_img + bias
    growth = jnp.exp(jnp.where(hit, -logits, logits))
    sig = growth / (1.0 + growth)
    return growth, jnp.where(hit, -sig, sig)


def softplus_sum(growth):
    parts = jnp.split(growth, 4, axis=0)
    while len(parts) > 1:
        parts = [a + b + a * b for a, b in zip(parts[::2], parts[1::2])]
    return jnp.sum(jnp.log1p(parts[0]), axis=0, keepdims=True)


def image_visit(scale, bias, block, xb, inv_img, positive, offset, inv_txt):
    raw = dot(block, xb, NN)
    growth, slope = meet(scale, bias, raw, inv_txt, inv_img, signs(positive, offset, raw.shape))
    weight = (slope * inv_txt).astype(jnp.bfloat16)
    along = jnp.sum(weight.astype(jnp.float32) * raw, axis=0, keepdims=True)
    return dot(weight, block, TN), softplus_sum(growth), along


def arrived_kernel(block_ref, out_ref):
    out_ref[...] = jnp.zeros(out_ref.shape, jnp.float32)


def norms_kernel(own_ref, back2_ref, out_ref):
    lanes = lax.broadcasted_iota(jnp.int32, out_ref.shape, 1)
    out_ref[...] = jnp.where(lanes == 0, inv_rows(own_ref[...]), inv_rows(back2_ref[...]))


def near_kernel(block_ref, out_ref):
    out_ref[...] = block_ref[...]


def pick_kernel(parity_ref, swap_ref, back1_ref, after_ref, prev_ref):
    prev_ref[...] = pick(parity_ref[0], swap_ref, back1_ref)


def early_kernel(log_scale_ref, bias_ref, image_ref, own_ref, back2_ref, norms_ref, acc_ref, loss_ref, along_ref):
    scale, bias = scale_of(log_scale_ref), bias_ref[0]
    xb, inv_img, positive = read_images(image_ref)
    part, loss, along = image_visit(scale, bias, own_ref[...], xb, inv_img, positive, 0, norms_ref[:, 0:1])
    acc_ref[...] = part
    part, loss2, along2 = image_visit(scale, bias, back2_ref[...], xb, inv_img, positive, 2, norms_ref[:, 1:2])
    acc_ref[...] += part
    loss_ref[...] = loss + loss2
    along_ref[...] = along + along2


def pick(odd, when_odd_ref, when_even_ref):
    return jnp.where(odd == 1, when_odd_ref[...], when_even_ref[...])


def late_kernel(
    per, log_scale_ref, bias_ref, image_ref, early_ref, early_loss_ref, early_along_ref, prev_ref,
    back3_ref, after_ref, loss_ref, grad_ref, acc_ref, x_ref,
):
    scale, bias = scale_of(log_scale_ref), bias_ref[0]
    xb, inv_img, positive = read_images(image_ref)
    prev = prev_ref[...]
    part, loss, along = image_visit(scale, bias, prev, xb, inv_img, positive, 1, inv_rows(prev))
    acc_ref[...] = early_ref[...] + part
    back3 = back3_ref[...]
    part, loss3, along3 = image_visit(scale, bias, back3, xb, inv_img, positive, 3, inv_rows(back3))
    acc_ref[...] += part
    loss_ref[...] = (early_loss_ref[...] + loss + loss3) * (1.0 / (STEPS * back3_ref.shape[0]))
    inner = (early_along_ref[...] + along + along3) * inv_img * inv_img
    x_ref[...] = (scale * inv_img) * (acc_ref[...].T - xb.astype(jnp.float32) * inner)
    repack(per, x_ref, grad_ref)


def text_visit(scale, bias, block, inv_txt, images, offset):
    xb, inv_img, positive = images
    raw = dot(block, xb, NN)
    slope = meet(scale, bias, raw, inv_txt, inv_img, signs(positive, offset, raw.shape))[1]
    return dot((slope * inv_img).astype(jnp.bfloat16), xb, NT)


def text_own_kernel(
    log_scale_ref, bias_ref, prev_ref, image_ref, after_ref, acc_ref, inv_ref
):
    scale, bias = scale_of(log_scale_ref), bias_ref[0]
    prev = prev_ref[...]
    inv_prev = inv_rows(prev)
    inv_ref[...] = inv_prev
    acc_ref[...] = text_visit(scale, bias, prev, inv_prev, read_images(image_ref), 1)


def text_send_kernel(log_scale_ref, bias_ref, prev_ref, inv_ref, acc_ref, img_next_ref, send_ref):
    scale, bias = scale_of(log_scale_ref), bias_ref[0]
    total = acc_ref[...] + text_visit(scale, bias, prev_ref[...], inv_ref[...], read_images(img_next_ref), 3)
    send_ref[...] = total.astype(jnp.bfloat16)


def text_local_kernel(log_scale_ref, bias_ref, own_ref, image_ref, img_next_ref, after_ref, local_ref):
    scale, bias = scale_of(log_scale_ref), bias_ref[0]
    own = own_ref[...]
    inv_own = inv_rows(own)
    local_ref[...] = text_visit(scale, bias, own, inv_own, read_images(image_ref), 0)
    local_ref[...] += text_visit(scale, bias, own, inv_own, read_images(img_next_ref), 2)


def finish_kernel(log_scale_ref, own_ref, got_ref, local_ref, after_ref, sent_ref, out_ref, grad_ref, out_sem):
    scale = scale_of(log_scale_ref)
    parts = out_sem.shape[0]
    rows = out_ref.shape[0] // parts

    def store(i):
        at = pl.ds(rows * i, rows)
        return pltpu.make_async_copy(grad_ref.at[at], out_ref.at[at], out_sem.at[i])

    for i in range(parts):
        at = pl.ds(rows * i, rows)
        own = own_ref[at]
        inv = inv_rows(own)
        y = own.astype(jnp.float32) * inv
        grad = scale * (got_ref[at].astype(jnp.float32) + local_ref[at])
        grad_ref[at] = inv * (grad - y * jnp.sum(y * grad, axis=1, keepdims=True))
        store(i).start()
    for i in range(parts):
        store(i).wait()


HBM = pl.BlockSpec(memory_space=pltpu.HBM)
SMEM = pl.BlockSpec(memory_space=pltpu.SMEM)
VMEM = pl.BlockSpec(memory_space=pltpu.VMEM)


def call(kernel, out_shape, in_specs, scratch, flops, moved, out_spec=None, limit=VMEM_BYTES):
    several = isinstance(out_shape, (list, tuple))
    return pl.pallas_call(
        kernel,
        out_shape=out_shape,
        in_specs=in_specs,
        out_specs=tuple(VMEM for _ in out_shape) if several else out_spec or VMEM,
        scratch_shapes=scratch,
        compiler_params=pltpu.CompilerParams(vmem_limit_bytes=limit),
        cost_estimate=pl.CostEstimate(flops=flops, bytes_accessed=moved, transcendentals=0),
    )


def shards(images, texts, positive, log_scale, bias):
    per = images.shape[0]
    rows, width = texts.shape
    ranks = lax.axis_size("mp")
    packed_rows = width * rows // LANES
    parity = lax.rem(lax.axis_index("batch"), 2).reshape((1,))
    place = positive.reshape((1, rows))
    flat = jax.ShapeDtypeStruct((packed_rows, LANES), jnp.bfloat16)
    block_bytes = rows * width * 2
    task = 2 * rows * rows * width

    square = jax.ShapeDtypeStruct((rows, width), jnp.float32)
    line = jax.ShapeDtypeStruct((1, rows), jnp.float32)
    block = jax.ShapeDtypeStruct((rows, width), jnp.bfloat16)
    tall = jax.ShapeDtypeStruct((width + TAIL, rows), jnp.bfloat16)

    back2 = hop(texts, 2)
    swapped = swap(texts)
    packed = call(functools.partial(pack_kernel, per), flat, [HBM], [
            pltpu.VMEM(images.shape, jnp.bfloat16),
            pltpu.VMEM(flat.shape, jnp.bfloat16),
            pltpu.SemaphoreType.DMA((PARTS,)),
            pltpu.SemaphoreType.DMA((PARTS,)),
        ], 0, 2 * block_bytes, HBM, 60 * 1024 * 1024)(images)
    back3 = hop(back2, 1)
    back1 = hop(swapped, 2, 0)

    packed = lax.all_to_all(packed, "mp", split_axis=0, concat_axis=0, tiled=True)
    column = jax.ShapeDtypeStruct((rows, 1), jnp.float32)
    tile = jax.ShapeDtypeStruct((8, LANES), jnp.float32)
    pair = jax.ShapeDtypeStruct((rows, LANES), jnp.float32)
    arrived = call(arrived_kernel, tile, [HBM], [], 10_000_000_000, block_bytes)(back2)
    near2 = call(near_kernel, block, [VMEM], [], 1_000_000_000, 2 * block_bytes)(back2)
    norms = call(norms_kernel, pair, [VMEM] * 2, [], 1_000_000_000, 2 * block_bytes)(texts, near2)
    image = call(functools.partial(gather_kernel, per), tall, [VMEM] * 3, [], 0, 2 * block_bytes)(
        packed, place, arrived
    )
    image_next = hop(image, -2)

    arrived3 = call(arrived_kernel, tile, [HBM], [], 1_000_000_000, block_bytes)(back3)
    prev = call(pick_kernel, block, [SMEM] + [VMEM] * 3, [], 0, 3 * block_bytes)(parity, swapped, back1, arrived3)
    early, early_loss, early_along = call(
        early_kernel, (square, line, line), [SMEM] * 2 + [VMEM] * 4, [], 4 * task, 5 * block_bytes
    )(log_scale, bias, image, texts, near2, norms)
    loss, grad = call(
        functools.partial(late_kernel, per),
        (line, flat),
        [SMEM] * 2 + [VMEM] * 6 + [HBM],
        [pltpu.VMEM((rows, width), jnp.float32), pltpu.VMEM((width, rows), jnp.float32)],
        4 * task,
        7 * block_bytes,
    )(log_scale, bias, image, early, early_loss, early_along, prev, back3, back1)
    image_grad = lax.all_to_all(grad, "mp", split_axis=0, concat_axis=0, tiled=True)

    text_own, inv_prev = call(
        text_own_kernel, (square, column), [SMEM] * 2 + [VMEM] * 3, [], 2 * task, 4 * block_bytes
    )(log_scale, bias, prev, image, loss)
    send = call(text_send_kernel, block, [SMEM] * 2 + [VMEM] * 4, [], 2 * task, 5 * block_bytes)(
        log_scale, bias, prev, inv_prev, text_own, image_next
    )
    got = hop(send, -1)
    local = call(text_local_kernel, square, [SMEM] * 2 + [VMEM] * 4, [], 4 * task, 5 * block_bytes)(
        log_scale, bias, texts, image, image_next, send
    )
    landed = call(arrived_kernel, tile, [HBM], [], 0, LANES)(got)
    text_grad = call(
        finish_kernel,
        square,
        [SMEM, VMEM, VMEM, VMEM, VMEM, HBM],
        [
            pltpu.VMEM((rows, width), jnp.float32),
            pltpu.SemaphoreType.DMA((PARTS,)),
        ],
        0,
        6 * block_bytes,
        HBM,
    )(log_scale, texts, got, local, landed, send)

    wide = jax.ShapeDtypeStruct((per, ranks * rows), jnp.bfloat16)
    image_grad = call(functools.partial(spread_kernel, per), wide, [VMEM], [], 0, 2 * block_bytes)(image_grad)
    return (loss.reshape((rows,)), image_grad, text_grad)


def solution(mesh):
    in_specs = (P("mp", "batch"), P(("batch", "mp"), None), P(("batch", "mp")), P(), P())
    out_specs = (P(("batch", "mp")), P("mp", "batch"), P(("batch", "mp"), None))
    return jax.shard_map(shards, mesh=mesh, in_specs=in_specs, out_specs=out_specs, check_vma=False)
```
